256 devices in a mesh: gx: 16 (over y, x_lo, core), gy: 16 (over z, x_hi).
Axes of the slice: x: 4 (x_hi: 2, x_lo: 2; x = x_hi * 2 + x_lo), y: 4, z: 8, core: 2. Of those that a mesh axis runs over, the one named last changes fastest.
Arguments:
- features: bfloat16 [128, 128, 2, 8, 256], P('gx', 'gy'), may hold values from -6 to 6
- cotangent: bfloat16 [128, 128, 2, 8, 256], P('gx', 'gy'), may hold values from -6 to 6
- weights: bfloat16 [27, 256, 256], replicated, may hold values from -0.078125 to 0.078125
- levels: int32 [16, 16, 2], P('gx', 'gy'), may hold values from 0 to 2, as said below
- counts: int32 [16, 16], P('gx', 'gy'), may hold values from 1 to 2, as said below
Outputs:
- output: bfloat16 [128, 128, 2, 8, 256], P('gx', 'gy')
- input_grad: bfloat16 [128, 128, 2, 8, 256], P('gx', 'gy')
- weight_grad: float32 [1769472], P(('gx', 'gy'))
The draws below stay inside these ranges and needn't reach their ends.
Inputs may be any that keep to these rules, and one draw needn't show every extreme that they name: `levels`: slot s of a tile sits at level s or s + 1, the same shift for all slots of that tile. The active slots of a tile are its first counts slots.
All inputs are finite; a program needn't handle non-finite values.
Results may differ from the reference program's by a relative error of at most 0.001.
Values may be sent and summed in bfloat16 or wider, within the bound.
A program may use at most 128 MiB of HBM per device.

```python
import math
import jax
import jax.numpy as jnp
import numpy as np
from jax import lax

C = 256
BLOCK = 8
NB = 2
X = 128
Y = 128
VOXELS = 262144
N_GX = 16
N_GY = 16


def draw_levels(key, part):
    key = jax.random.fold_in(key, 11)
    ground_shift = jax.random.randint(key, (N_GX, N_GY), 0, 2).astype(jnp.int32)
    ground_shift = ground_shift.at[0, 0].set(1).at[0, 1].set(0)
    return ground_shift[:, :, None] + jnp.arange(NB, dtype=jnp.int32)[None, None, :]


def draw_counts(key, part):
    key = jax.random.fold_in(key, 23)
    tile_counts = jax.random.randint(key, (N_GX, N_GY), 1, NB + 1).astype(jnp.int32)
    return tile_counts.at[0, 0].set(NB).at[1, 1].set(1)


def steps_of(rng, dims, split, low, high):
    def one(dim, parts):
        heights = jax.random.uniform(jax.random.fold_in(jax.random.fold_in(rng, 6), dim), (parts,), jnp.float32, low / len(split), high / len(split))
        return jnp.repeat(jnp.exp(heights), dims[dim] // parts).reshape((-1,) + (1,) * (len(dims) - dim - 1))

    loudness = one(*split[0])
    for cut in split[1:]:
        loudness = loudness * one(*cut)
    return loudness


def scatter_about(rng, dims, scale, bound, pieces=(), held_as=jnp.bfloat16):
    result = scale * jax.random.normal(rng, dims, jnp.float32)
    if pieces:
        result = result * steps_of(rng, dims, pieces, -0.22, 0.18)
    return jnp.clip(result, -bound, bound).astype(held_as)


def setup_inputs(seed: int = 0) -> dict:
    seeds = jax.random.split(jax.random.key(seed), 6)
    features = scatter_about(seeds[0], (X, Y, NB, BLOCK, C), 1.0, 6.0, ((0, 16), (1, 16)))
    cotangent = scatter_about(seeds[1], (X, Y, NB, BLOCK, C), 1.0, 6.0, ((0, 16), (1, 16)))
    weights = scatter_about(seeds[2], (27, C, C), (27 * C) ** -0.5, 0.078125)
    levels = draw_levels(jax.random.fold_in(seeds[5], 71), 0)
    counts = draw_counts(jax.random.fold_in(seeds[5], 71), 0)
    return dict(features=features, cotangent=cotangent, weights=weights, levels=levels, counts=counts)


def assemble(window, near_levels, own_levels):
    extent = window.shape[0]
    column_map = np.array([0] + [1] * (extent - 2) + [2], dtype=np.int32)
    spread = near_levels[column_map][:, column_map]
    targets = own_levels[:, None] + jnp.array([-1, 0, 1], dtype=jnp.int32)[None, :]
    selector = (spread[:, :, None, None, :] == targets[None, None, :, :, None]).astype(jnp.float32)
    stacked = jnp.einsum('ijskr,ijrzc->ijskzc', selector, window.astype(jnp.float32))
    below_layer = stacked[:, :, :, 0, -1:, :]
    same_level = stacked[:, :, :, 1]
    above_layer = stacked[:, :, :, 2, :1, :]
    return jnp.concatenate([below_layer, same_level, above_layer], axis=3).astype(jnp.bfloat16)

def convolve(frame, kernel, flipped):
    blocks = frame.shape[0] - 2
    frame_wide = frame.astype(jnp.float32)
    kernel_wide = kernel.astype(jnp.float32)
    summed = None
    for offset in range(27):
        step_x, step_y, step_z = (offset // 9, offset // 3 % 3, offset % 3)
        if flipped:
            step_x, step_y, step_z = (2 - step_x, 2 - step_y, 2 - step_z)
        sliced = frame_wide[step_x:step_x + blocks, step_y:step_y + blocks, :, step_z:step_z + blocks, :]
        if flipped:
            product = jnp.einsum('xyszc,dc->xyszd', sliced, kernel_wide[offset])
        else:
            product = jnp.einsum('xyszc,cd->xyszd', sliced, kernel_wide[offset])
        summed = product if summed is None else summed + product
    return summed

def weight_terms(frame, grads):
    blocks = grads.shape[0]
    frame_wide = frame.astype(jnp.float32)
    grads_wide = grads.astype(jnp.float32)
    terms = []
    for offset in range(27):
        step_x, step_y, step_z = (offset // 9, offset // 3 % 3, offset % 3)
        sliced = frame_wide[step_x:step_x + blocks, step_y:step_y + blocks, :, step_z:step_z + blocks, :]
        terms.append(jnp.einsum('xyszc,xyszd->cd', sliced, grads_wide))
    return jnp.stack(terms)

def reference(features, cotangent, weights, levels, counts):
    blocks = BLOCK
    slot_ids = jnp.arange(NB, dtype=jnp.int32)
    active = slot_ids[None, None, :] < counts[:, :, None]
    effective = jnp.where(active, levels, jnp.full_like(levels, -1000))
    level_pad = jnp.pad(effective, ((1, 1), (1, 1), (0, 0)))
    active_vox = jnp.repeat(jnp.repeat(active, blocks, axis=0), blocks, axis=1)[:, :, :, None, None]
    masked_cot = jnp.where(active_vox, cotangent, jnp.zeros_like(cotangent))
    pads = ((1, 1), (1, 1), (0, 0), (0, 0), (0, 0))
    feat_pad = jnp.pad(features, pads)
    cot_pad = jnp.pad(masked_cot, pads)
    zero_index = jnp.zeros((), jnp.int32)

    def tile(carry, tile_index):
        tile_row = (tile_index // N_GY).astype(jnp.int32)
        tile_col = (tile_index % N_GY).astype(jnp.int32)
        starts = (tile_row * blocks, tile_col * blocks, zero_index, zero_index, zero_index)
        sizes = (blocks + 2, blocks + 2, NB, blocks, C)
        window_x = lax.dynamic_slice(feat_pad, starts, sizes)
        window_g = lax.dynamic_slice(cot_pad, starts, sizes)
        near_levels = lax.dynamic_slice(level_pad, (tile_row, tile_col, zero_index), (3, 3, NB))
        own_levels = near_levels[1, 1]
        frame_x = assemble(window_x, near_levels, own_levels)
        frame_g = assemble(window_g, near_levels, own_levels)
        keep_mask = (slot_ids < counts[tile_row, tile_col])[None, None, :, None, None]
        out_tile = jnp.where(keep_mask, convolve(frame_x, weights, False), 0.0).astype(jnp.bfloat16)
        back_tile = jnp.where(keep_mask, convolve(frame_g, weights, True), 0.0).astype(jnp.bfloat16)
        carry = carry + weight_terms(frame_x, window_g[1:-1, 1:-1])
        return (carry, (out_tile, back_tile))
    start_carry = jnp.zeros((27, C, C), jnp.float32)
    total, (out_tiles, back_tiles) = lax.scan(tile, start_carry, jnp.arange(N_GX * N_GY, dtype=jnp.int32))

    def place(tiles):
        shaped = tiles.reshape(N_GX, N_GY, blocks, blocks, NB, blocks, C)
        return shaped.transpose(0, 2, 1, 3, 4, 5, 6).reshape(N_GX * blocks, N_GY * blocks, NB, blocks, C)
    grad_scale = 1.0 / math.sqrt(VOXELS)
    weight_grad = (total * grad_scale).reshape(-1)
    return (place(out_tiles), place(back_tiles), weight_grad)
```

```python
import functools
import math

import jax
import jax.numpy as jnp
from jax import lax
from jax.experimental import pallas as pl
from jax.experimental.pallas import tpu as pltpu
from jax.sharding import PartitionSpec as P

F32 = jnp.float32
BF16 = jnp.bfloat16
MESH = pl.DeviceIdType.MESH

DIRS = ((-1, 0), (1, 0), (0, -1), (0, 1), (-1, -1), (-1, 1), (1, -1), (1, 1))
COLS = (0, 8, 16, 24, 32, 33, 34, 35)
WIDE = (8, 8, 8, 8, 1, 1, 1, 1)
ENDS = (8, 15, 21, 27)
HALF = 216
PADDED = 224
UNIT = 32000.0


def up_down(v, top, bottom, z):
    rows = v.shape[0]
    lower = jnp.where(z == 0, bottom, pltpu.roll(v, 1, 0))
    higher = jnp.where(z == 15, top, pltpu.roll(v, rows - 1, 0))
    return lower, higher


def exponent(v):
    peak = jnp.max(jnp.abs(v), axis=0, keepdims=True)
    return jnp.ceil(jnp.log2(jnp.maximum(peak, 1e-30)))


def encode(v):
    k = exponent(v)
    q = jnp.floor(v * (jnp.exp2(-k) * UNIT) + 0.5)
    tail = jnp.broadcast_to(k, (PADDED - HALF, v.shape[1]))
    return jnp.concatenate([q, tail], axis=0).astype(jnp.int32).astype(jnp.int16)


def decode(q):
    w = q.astype(jnp.int32).astype(F32)
    return w[:HALF] * (jnp.exp2(w[HALF : HALF + 1]) * (1.0 / UNIT))


def kernel(
    scale, lev, cnt, f_hbm, g_hbm, w_hbm, out_ref, ig_ref, wg_ref,
    f_own, g_own, w_all, f_fr, g_fr, f_halo, g_halo, meta, near, ft, wg,
    r0, qx1, qy1, ownx, owny, rx1, ry1, qx2, qy2, rx2, ry2, total, q3, r3,
    load_sem, hs, hr, s0s, s0r, x1s, x1r, y1s, y1r, x2s, x2r, y2s, y2r, s3s, s3r,
):
    gx, gy = lax.axis_index("gx"), lax.axis_index("gy")
    y, xl, core = lax.div(gx, 4), lax.rem(lax.div(gx, 2), 2), lax.rem(gx, 2)
    z, xh = lax.div(gy, 2), lax.rem(gy, 2)
    x = xh * 2 + xl

    def place(y_, x_, core_, z_):
        return (y_ * 4 + lax.rem(x_, 2) * 2 + core_, z_ * 2 + lax.div(x_, 2))

    sibling = place(y, x, 1 - core, z)

    def x_peer(j):
        return lax.rem(x + j, 4)

    def y_peer(j):
        return lax.rem(y + j, 4)

    def neighbour(d):
        return (lax.rem(gx + d[0] + 16, 16), lax.rem(gy + d[1] + 16, 16))

    loads = [
        pltpu.make_async_copy(g_hbm, g_own, load_sem.at[0]),
        pltpu.make_async_copy(f_hbm, f_own, load_sem.at[1]),
        pltpu.make_async_copy(w_hbm, w_all, load_sem.at[2]),
    ]
    for c in loads:
        c.start()

    own_source = lax.div(z, 4) == xh
    barrier = pltpu.get_barrier_semaphore()
    for d in DIRS:
        pl.semaphore_signal(barrier, inc=1, device_id=neighbour(d), device_id_type=MESH)
    pl.semaphore_signal(barrier, inc=1, device_id=sibling, device_id_type=MESH)
    for j in (1, 2, 3):
        pl.semaphore_signal(barrier, inc=1, device_id=place(y, x_peer(j), core, z), device_id_type=MESH)
        pl.semaphore_signal(barrier, inc=1, device_id=place(y_peer(j), x, core, z), device_id_type=MESH)
    source_x = lax.div(z, 4) * 2 + xl
    for s in range(8):

        @pl.when(jnp.logical_not(jnp.logical_and(own_source, z == s)))
        def _():
            pl.semaphore_signal(barrier, inc=1, device_id=place(y, source_x, core, s), device_id_type=MESH)

    shift = lev[0, 0, 0].astype(F32)
    second = jnp.where(cnt[0, 0] >= 2, 1.0, 0.0).astype(F32)
    eight = lax.broadcasted_iota(jnp.int32, (8, 256), 0)
    meta[...] = jnp.where(eight < 4, shift, second)
    loads[0].wait()
    loads[1].wait()
    pl.semaphore_wait(barrier, 23 - own_source.astype(jnp.int32))

    def edge(ref, d):
        row = {-1: 0, 1: 7}
        if d[0] and d[1]:
            return ref.at[row[d[0]], row[d[1]]]
        return ref.at[row[d[0]]] if d[0] else ref.at[:, row[d[1]]]

    def slot(ref, i):
        return ref.at[COLS[i]] if WIDE[i] == 1 else ref.at[pl.ds(COLS[i], 8)]

    def halo(kind, i):
        d = DIRS[i]
        opposite = DIRS.index((-d[0], -d[1]))
        if kind == 0:
            src, dst = meta, near.at[opposite]
        else:
            src = edge((None, g_own, f_own)[kind], d)
            dst = slot((None, g_halo, f_halo)[kind], opposite)
        return pltpu.make_async_remote_copy(
            src_ref=src, dst_ref=dst, send_sem=hs.at[kind, i], recv_sem=hr.at[kind, opposite],
            device_id=neighbour(d), device_id_type=MESH,
        )

    started = []

    def go(copy):
        copy.start()
        started.append(copy)

    for kind in range(3):
        for i in range(8):
            go(halo(kind, i))

    def z_of(rows):
        return lax.rem(lax.broadcasted_iota(jnp.int32, (rows, 256), 0), 16)

    z128 = z_of(128)
    keep128 = jnp.where(z128 < 8, 1.0, second)

    def own_columns(src, fr, with_transpose):
        for r in range(8):
            v = src[r].reshape(128, 256).astype(F32) * keep128
            lower, higher = up_down(v, 0.0, 0.0, z128)
            for k, t in enumerate((lower, v, higher)):
                fr[k, r + 1, 1:9] = t.astype(BF16).reshape(8, 16, 256)
            if with_transpose:
                ft[:, r * 128 : (r + 1) * 128] = v.T.astype(BF16)

    own_columns(g_own, g_fr, False)
    own_columns(f_own, f_fr, True)

    def near_columns(kind, recv, fr):
        for i, (dx, dy) in enumerate(DIRS):
            if kind == 1:
                halo(0, DIRS.index((-dx, -dy))).wait_recv()
            halo(kind, DIRS.index((-dx, -dy))).wait_recv()
            n = WIDE[i]
            inside = jnp.logical_and(
                jnp.logical_and(gx + dx >= 0, gx + dx < 16), jnp.logical_and(gy + dy >= 0, gy + dy < 16)
            )
            valid = jnp.where(inside, 1.0, 0.0).astype(F32)
            higher_by = near[i, 0:1, :] - shift
            level = jnp.where(higher_by == 0.0, valid, 0.0)
            above = jnp.where(higher_by == 1.0, valid, 0.0)
            below = jnp.where(higher_by == -1.0, valid, 0.0)
            rows = n * 16
            zr = z_of(rows)
            v = recv[COLS[i] : COLS[i] + n].reshape(rows, 256).astype(F32)
            v = v * jnp.where(zr < 8, 1.0, near[i, 4:5, :])
            swapped = pltpu.roll(v, 8, 0) if n == 1 else None
            up8 = swapped if n == 1 else pltpu.roll(v, 8, 0)
            down8 = swapped if n == 1 else pltpu.roll(v, rows - 8, 0)
            c = level * v + jnp.where(zr >= 8, above * up8, below * down8)
            top = above * pltpu.roll(v, 7, 0)
            bottom = below * pltpu.roll(v, rows - 7, 0)
            lower, higher = up_down(c, top, bottom, zr)
            xs = {-1: 0, 0: slice(1, 9), 1: 9}[dx]
            ys = {-1: 0, 0: slice(1, 9), 1: 9}[dy]
            for k, t in enumerate((lower, c, higher)):
                t = t.astype(BF16)
                fr[k, xs, ys] = t if n == 1 else t.reshape(8, 16, 256)

    near_columns(1, g_halo, g_fr)

    first = y_peer(1)
    base = lax.div(27 * first, 4)

    def gradient(i):
        o = lax.rem(base + i, 27)
        dx, dy, dz = lax.div(o, 9), lax.rem(lax.div(o, 3), 3), lax.rem(o, 3)
        g = g_fr[2 - dz, pl.ds(2 - dx, 8), pl.ds(2 - dy, 8)].reshape(1024, 256)
        wg[pl.ds(pl.multiple_of(o * 256, 256), 256), :] = jnp.dot(ft[...], g, preferred_element_type=F32)

    def phase_y(p):
        return lax.rem(y + 1 + p, 4)

    def rows_of(p, xl_, core_):
        return pl.multiple_of(((phase_y(p) * 2 + xl_) * 2 + core_) * (2 * HALF), 8)

    def send0(p):
        for a in range(2):
            go(pltpu.make_async_remote_copy(
                src_ref=wg.at[pl.ds(rows_of(p, a, 1 - core), 2 * HALF)], dst_ref=r0.at[p, a],
                send_sem=s0s.at[p, a], recv_sem=s0r.at[p, a], device_id=sibling, device_id_type=MESH,
            ))

    def copy_x1(p, j):
        return pltpu.make_async_remote_copy(
            src_ref=qx1.at[p, j - 1], dst_ref=rx1.at[p, j - 1], send_sem=x1s.at[p, j - 1],
            recv_sem=x1r.at[p, j - 1], device_id=place(y, x_peer(j), core, z), device_id_type=MESH,
        )

    def copy_y1(p):
        return pltpu.make_async_remote_copy(
            src_ref=qy1.at[p], dst_ref=ry1.at[p], send_sem=y1s.at[p], recv_sem=y1r.at[p],
            device_id=place(phase_y(p), x, core, z), device_id_type=MESH,
        )

    def send1(p):
        for a in range(2):
            pltpu.make_async_remote_copy(
                src_ref=wg.at[pl.ds(rows_of(p, a, 1 - core), 2 * HALF)], dst_ref=r0.at[p, a],
                send_sem=s0s.at[p, a], recv_sem=s0r.at[p, a], device_id=sibling, device_id_type=MESH,
            ).wait_recv()
        for a in range(2):
            for h in range(2):
                mine = wg[pl.ds(pl.multiple_of(rows_of(p, a, core) + h * HALF, 8), HALF), 128:256]
                v = mine + r0[p, a, h * HALF : (h + 1) * HALF, 128:256]
                if p < 3:
                    qy1[p, a * 2 + h] = encode(v)
                else:
                    owny[a * 2 + h] = v
        if p < 3:
            go(copy_y1(p))
        for j in (2, 1, 3, 0):
            to = x_peer(j)
            a, h = lax.rem(to, 2), lax.div(to, 2)
            mine = wg[pl.ds(pl.multiple_of(rows_of(p, a, core) + h * HALF, 8), HALF), 0:128]
            v = mine + r0[p, a, pl.ds(pl.multiple_of(h * HALF, 8), HALF), 0:128]
            if j:
                qx1[p, j - 1] = encode(v)
                go(copy_x1(p, j))
            else:
                ownx[p] = v

    def copy_x2(p):
        return pltpu.make_async_remote_copy(
            src_ref=qx2.at[p], dst_ref=rx2.at[p], send_sem=x2s.at[p], recv_sem=x2r.at[p],
            device_id=place(phase_y(p), x, core, z), device_id_type=MESH,
        )

    def copy_y2(j):
        return pltpu.make_async_remote_copy(
            src_ref=qy2.at[j - 1], dst_ref=ry2.at[j - 1], send_sem=y2s.at[j - 1], recv_sem=y2r.at[j - 1],
            device_id=place(y, x_peer(j), core, z), device_id_type=MESH,
        )

    def send2x(p):
        v = ownx[p]
        for j in (1, 2, 3):
            copy_x1(p, j).wait_recv()
            v = v + decode(rx1[p, j - 1])
        if p < 3:
            qx2[p] = encode(v)
            go(copy_x2(p))
        else:
            total[0:HALF, 0:128] = v

    def send2y():
        for p in range(3):
            copy_y1(p).wait_recv()
        for j in (2, 1, 3, 0):
            to = x_peer(j)
            i = lax.rem(to, 2) * 2 + lax.div(to, 2)
            v = owny[i]
            for p in range(3):
                v = v + decode(ry1[p, i])
            if j:
                qy2[j - 1] = encode(v)
                go(copy_y2(j))
            else:
                total[0:HALF, 128:256] = v

    row32 = lax.broadcasted_iota(jnp.int32, (32, 256), 0)

    def copy_3(j):
        return pltpu.make_async_remote_copy(
            src_ref=q3.at[j], dst_ref=r3.at[z], send_sem=s3s.at[j], recv_sem=s3r.at[z],
            device_id=place(y, (j % 2) * 2 + xl, core, xh * 4 + j // 2), device_id_type=MESH,
        )

    def is_self(j):
        return jnp.logical_and(own_source, lax.rem(z, 4) * 2 + xh == j)

    def send3():
        v = total[0:HALF, 0:128]
        for p in range(3):
            copy_x2(p).wait_recv()
            v = v + decode(rx2[p])
        total[0:HALF, 0:128] = v
        v = total[0:HALF, 128:256]
        for j in (1, 2, 3):
            copy_y2(j).wait_recv()
            v = v + decode(ry2[j - 1])
        total[0:HALF, 128:256] = v
        total[HALF:PADDED, :] = jnp.zeros((PADDED - HALF, 256), F32)
        for j in range(8):
            v = jnp.where(row32 < 27, total[27 * j : 27 * j + 32, :], 0.0)
            k = exponent(v)
            q = jnp.floor(v * (jnp.exp2(-k) * UNIT) + 0.5)
            q3[j] = jnp.where(row32 < 27, q, k).astype(jnp.int32).astype(jnp.int16)

            @pl.when(jnp.logical_not(is_self(j)))
            def _():
                copy_3(j).start()

            @pl.when(is_self(j))
            def _():
                r3[z] = q3[j]

    def finish():
        v = jnp.zeros((32, 256), F32)
        for s in range(8):

            @pl.when(jnp.logical_not(jnp.logical_and(own_source, z == s)))
            def _():
                pltpu.make_async_remote_copy(
                    src_ref=q3.at[s], dst_ref=r3.at[s], send_sem=s3s.at[s], recv_sem=s3r.at[s],
                    device_id=place(y, source_x, core, s), device_id_type=MESH,
                ).wait_recv()

            w = r3[s].astype(jnp.int32).astype(F32)
            v = v + w * (jnp.exp2(w[31:32]) * (1.0 / UNIT))
        wg_ref[...] = (v * scale)[:27]

    keep256 = jnp.where(z_of(256) < 8, 1.0, second)

    def convolve(fr, dst, transposed, lo, hi):
        def tile(t, _):
            acc = None
            for o in range(27):
                dx, dy, dz = o // 9, o // 3 % 3, o % 3
                a = fr[dz, pl.ds(2 * t + dx, 2), pl.ds(dy, 8)].reshape(256, 256)
                if transposed:
                    term = lax.dot_general(
                        a, w_all[26 - o], (((1,), (1,)), ((), ())), preferred_element_type=F32
                    )
                else:
                    term = jnp.dot(a, w_all[o], preferred_element_type=F32)
                acc = term if acc is None else acc + term
            dst[pl.ds(2 * t, 2)] = (acc * keep256).astype(BF16).reshape(2, 8, 16, 256)
            return 0

        lax.fori_loop(lo, hi, tile, 0)

    done = 0
    for p in range(4):
        for i in range(done, ENDS[p]):
            gradient(i)
        done = ENDS[p]
        send0(p)
        if p:
            send1(p - 1)
    near_columns(2, f_halo, f_fr)
    loads[2].wait()
    convolve(f_fr, out_ref, False, 0, 1)
    send1(3)
    convolve(f_fr, out_ref, False, 1, 4)
    send2x(0)
    send2x(1)
    convolve(g_fr, ig_ref, True, 0, 2)
    send2x(2)
    send2y()
    send2x(3)
    convolve(g_fr, ig_ref, True, 2, 4)
    send3()
    finish()
    for c in started:
        c.wait_send()
    for j in range(8):

        @pl.when(jnp.logical_not(is_self(j)))
        def _():
            copy_3(j).wait_send()


def per_device(features, cotangent, weights, levels, counts):
    f = features.reshape(8, 8, 16, 256)
    g = cotangent.reshape(8, 8, 16, 256)
    scale = 1.0 / math.sqrt(1024 * lax.axis_size("gx") * lax.axis_size("gy"))
    vmem = pl.BlockSpec(memory_space=pltpu.VMEM)
    smem = pl.BlockSpec(memory_space=pltpu.SMEM)
    anywhere = pl.BlockSpec(memory_space=pl.ANY)
    dma = pltpu.SemaphoreType.DMA
    i16 = jnp.int16
    out, ig, wgrad = pl.pallas_call(
        functools.partial(kernel, scale),
        out_shape=(
            jax.ShapeDtypeStruct((8, 8, 16, 256), BF16),
            jax.ShapeDtypeStruct((8, 8, 16, 256), BF16),
            jax.ShapeDtypeStruct((27, 256), F32),
        ),
        in_specs=[smem, smem, anywhere, anywhere, anywhere],
        out_specs=(vmem, vmem, vmem),
        scratch_shapes=[
            pltpu.VMEM((8, 8, 16, 256), BF16),
            pltpu.VMEM((8, 8, 16, 256), BF16),
            pltpu.VMEM((27, 256, 256), BF16),
            pltpu.VMEM((3, 10, 10, 16, 256), BF16),
            pltpu.VMEM((3, 10, 10, 16, 256), BF16),
            pltpu.VMEM((36, 16, 256), BF16),
            pltpu.VMEM((36, 16, 256), BF16),
            pltpu.VMEM((8, 256), F32),
            pltpu.VMEM((8, 8, 256), F32),
            pltpu.VMEM((256, 1024), BF16),
            pltpu.VMEM((6912, 256), F32),
            pltpu.VMEM((4, 2, 2 * HALF, 256), F32),
            pltpu.VMEM((4, 3, PADDED, 128), i16),
            pltpu.VMEM((3, 4, PADDED, 128), i16),
            pltpu.VMEM((4, HALF, 128), F32),
            pltpu.VMEM((4, HALF, 128), F32),
            pltpu.VMEM((4, 3, PADDED, 128), i16),
            pltpu.VMEM((3, 4, PADDED, 128), i16),
            pltpu.VMEM((3, PADDED, 128), i16),
            pltpu.VMEM((3, PADDED, 128), i16),
            pltpu.VMEM((3, PADDED, 128), i16),
            pltpu.VMEM((3, PADDED, 128), i16),
            pltpu.VMEM((PADDED, 256), F32),
            pltpu.VMEM((8, 32, 256), i16),
            pltpu.VMEM((8, 32, 256), i16),
            dma((3,)),
            dma((3, 8)),
            dma((3, 8)),
            dma((4, 2)),
            dma((4, 2)),
            dma((4, 3)),
            dma((4, 3)),
            dma((3,)),
            dma((3,)),
            dma((3,)),
            dma((3,)),
            dma((3,)),
            dma((3,)),
            dma((8,)),
            dma((8,)),
        ],
        compiler_params=pltpu.CompilerParams(
            collective_id=0, has_side_effects=True, vmem_limit_bytes=56 * 1024 * 1024
        ),
    )(levels, counts, f, g, weights)
    shape = features.shape
    return out.reshape(shape), ig.reshape(shape), wgrad.reshape(-1)


def solution(mesh):
    return jax.shard_map(
        per_device,
        mesh=mesh,
        in_specs=(
            P("gx", "gy", None, None, None),
            P("gx", "gy", None, None, None),
            P(),
            P("gx", "gy", None),
            P("gx", "gy"),
        ),
        out_specs=(
            P("gx", "gy", None, None, None),
            P("gx", "gy", None, None, None),
            P(("gx", "gy")),
        ),
        check_vma=False,
    )
```

```python
import functools
import math

import jax
import jax.numpy as jnp
from jax import lax
from jax.experimental import pallas as pl
from jax.experimental.pallas import tpu as pltpu
from jax.sharding import PartitionSpec as P

F32 = jnp.float32
BF16 = jnp.bfloat16
MESH = pl.DeviceIdType.MESH

DIRS = ((-1, 0), (1, 0), (0, -1), (0, 1), (-1, -1), (-1, 1), (1, -1), (1, 1))
COLS = (0, 8, 16, 24, 32, 33, 34, 35)
WIDE = (8, 8, 8, 8, 1, 1, 1, 1)
PHASES = tuple((p, a) for p in range(4) for a in range(2))
ENDS = (5, 8, 11, 15, 18, 21, 25, 27)
SHARE = 27
HALF = 8 * SHARE
PADDED = 224
UNIT = 32000.0


def up_down(v, top, bottom, z):
    rows = v.shape[0]
    lower = jnp.where(z == 0, bottom, pltpu.roll(v, 1, 0))
    higher = jnp.where(z == 15, top, pltpu.roll(v, rows - 1, 0))
    return lower, higher


def exponent(v):
    peak = jnp.max(jnp.abs(v), axis=0, keepdims=True)
    return jnp.ceil(jnp.log2(jnp.maximum(peak, 1e-30)))


def encode(v):
    k = exponent(v)
    q = jnp.floor(v * (jnp.exp2(-k) * UNIT) + 0.5)
    tail = jnp.broadcast_to(k, (PADDED - HALF, v.shape[1]))
    return jnp.concatenate([q, tail], axis=0).astype(jnp.int32).astype(jnp.int16)


def decode(q):
    w = q.astype(jnp.int32).astype(F32)
    return w[:HALF] * (jnp.exp2(w[HALF : HALF + 1]) * (1.0 / UNIT))


def kernel(
    scale, lev, cnt, f_hbm, g_hbm, w_hbm, out_ref, ig_ref, wg_ref,
    f_own, g_own, w_all, f_fr, g_fr, f_halo, g_halo, meta, near, ft, wg,
    r0, pair, parted, qx1, qy1, ownx, owny, rx1, ry1, qx2, qy2, rx2, ry2, total, q3, r3,
    load_sem, hs, hr, s0s, s0r, x1s, x1r, y1s, y1r, x2s, x2r, y2s, y2r, s3s, s3r,
):
    gx, gy = lax.axis_index("gx"), lax.axis_index("gy")
    y, xl, core = lax.div(gx, 4), lax.rem(lax.div(gx, 2), 2), lax.rem(gx, 2)
    z, xh = lax.div(gy, 2), lax.rem(gy, 2)
    x = xh * 2 + xl

    def place(y_, x_, core_, z_):
        return (y_ * 4 + lax.rem(x_, 2) * 2 + core_, z_ * 2 + lax.div(x_, 2))

    sibling = place(y, x, 1 - core, z)

    def x_peer(j):
        return lax.rem(x + j, 4)

    def y_peer(j):
        return lax.rem(y + j, 4)

    def z_peer(j):
        return lax.rem(z + j, 8)

    def neighbour(d):
        return (lax.rem(gx + d[0] + 16, 16), lax.rem(gy + d[1] + 16, 16))

    loads = [
        pltpu.make_async_copy(g_hbm, g_own, load_sem.at[0]),
        pltpu.make_async_copy(f_hbm, f_own, load_sem.at[1]),
        pltpu.make_async_copy(w_hbm, w_all, load_sem.at[2]),
    ]
    for c in loads:
        c.start()

    barrier = pltpu.get_barrier_semaphore()
    for d in DIRS:
        pl.semaphore_signal(barrier, inc=1, device_id=neighbour(d), device_id_type=MESH)
    pl.semaphore_signal(barrier, inc=1, device_id=sibling, device_id_type=MESH)
    for j in (1, 2, 3):
        pl.semaphore_signal(barrier, inc=1, device_id=place(y, x_peer(j), core, z), device_id_type=MESH)
        pl.semaphore_signal(barrier, inc=1, device_id=place(y_peer(j), x, core, z), device_id_type=MESH)
    for j in range(1, 8):
        pl.semaphore_signal(barrier, inc=1, device_id=place(y, x, core, z_peer(j)), device_id_type=MESH)

    shift = lev[0, 0, 0].astype(F32)
    second = jnp.where(cnt[0, 0] >= 2, 1.0, 0.0).astype(F32)
    eight = lax.broadcasted_iota(jnp.int32, (8, 256), 0)
    meta[...] = jnp.where(eight < 4, shift, second)
    loads[0].wait()
    loads[1].wait()
    pl.semaphore_wait(barrier, 22)

    def edge(ref, d):
        row = {-1: 0, 1: 7}
        if d[0] and d[1]:
            return ref.at[row[d[0]], row[d[1]]]
        return ref.at[row[d[0]]] if d[0] else ref.at[:, row[d[1]]]

    def slot(ref, i):
        return ref.at[COLS[i]] if WIDE[i] == 1 else ref.at[pl.ds(COLS[i], 8)]

    def halo(kind, i):
        d = DIRS[i]
        opposite = DIRS.index((-d[0], -d[1]))
        if kind == 0:
            src, dst = meta, near.at[opposite]
        else:
            src = edge((None, g_own, f_own)[kind], d)
            dst = slot((None, g_halo, f_halo)[kind], opposite)
        return pltpu.make_async_remote_copy(
            src_ref=src, dst_ref=dst, send_sem=hs.at[kind, i], recv_sem=hr.at[kind, opposite],
            device_id=neighbour(d), device_id_type=MESH,
        )

    started = []

    def go(copy):
        copy.start()
        started.append(copy)

    for kind in range(2):
        for i in range(8):
            go(halo(kind, i))

    def z_of(rows):
        return lax.rem(lax.broadcasted_iota(jnp.int32, (rows, 256), 0), 16)

    z128 = z_of(128)
    keep128 = jnp.where(z128 < 8, 1.0, second)

    def own_columns(src, fr, with_transpose):
        for r in range(8):
            v = src[r].reshape(128, 256).astype(F32) * keep128
            lower, higher = up_down(v, 0.0, 0.0, z128)
            for k, t in enumerate((lower, v, higher)):
                fr[k, r + 1, 1:9] = t.astype(BF16).reshape(8, 16, 256)
            if with_transpose:
                ft[:, r * 128 : (r + 1) * 128] = v.T.astype(BF16)

    own_columns(g_own, g_fr, False)
    own_columns(f_own, f_fr, True)

    def near_columns(kind, recv, fr):
        for i, (dx, dy) in enumerate(DIRS):
            if kind == 1:
                halo(0, DIRS.index((-dx, -dy))).wait_recv()
            halo(kind, DIRS.index((-dx, -dy))).wait_recv()
            n = WIDE[i]
            inside = jnp.logical_and(
                jnp.logical_and(gx + dx >= 0, gx + dx < 16), jnp.logical_and(gy + dy >= 0, gy + dy < 16)
            )
            valid = jnp.where(inside, 1.0, 0.0).astype(F32)
            higher_by = near[i, 0:1, :] - shift
            level = jnp.where(higher_by == 0.0, valid, 0.0)
            above = jnp.where(higher_by == 1.0, valid, 0.0)
            below = jnp.where(higher_by == -1.0, valid, 0.0)
            rows = n * 16
            zr = z_of(rows)
            v = recv[COLS[i] : COLS[i] + n].reshape(rows, 256).astype(F32)
            v = v * jnp.where(zr < 8, 1.0, near[i, 4:5, :])
            swapped = pltpu.roll(v, 8, 0) if n == 1 else None
            up8 = swapped if n == 1 else pltpu.roll(v, 8, 0)
            down8 = swapped if n == 1 else pltpu.roll(v, rows - 8, 0)
            c = level * v + jnp.where(zr >= 8, above * up8, below * down8)
            top = above * pltpu.roll(v, 7, 0)
            bottom = below * pltpu.roll(v, rows - 7, 0)
            lower, higher = up_down(c, top, bottom, zr)
            xs = {-1: 0, 0: slice(1, 9), 1: 9}[dx]
            ys = {-1: 0, 0: slice(1, 9), 1: 9}[dy]
            for k, t in enumerate((lower, c, higher)):
                t = t.astype(BF16)
                fr[k, xs, ys] = t if n == 1 else t.reshape(8, 16, 256)

    near_columns(1, g_halo, g_fr)
    for i in range(8):
        go(halo(2, i))

    first = y_peer(1)
    base = lax.div(27 * first, 4)

    def gradient(i):
        o = lax.rem(base + i, 27)
        dx, dy, dz = lax.div(o, 9), lax.rem(lax.div(o, 3), 3), lax.rem(o, 3)
        g = g_fr[2 - dz, pl.ds(2 - dx, 8), pl.ds(2 - dy, 8)].reshape(1024, 256)
        wg[pl.ds(pl.multiple_of(o * 256, 256), 256), :] = jnp.dot(ft[...], g, preferred_element_type=F32)

    def phase_y(p):
        return lax.rem(y + 1 + p, 4)

    def rows_of(p, xl_, core_):
        return pl.multiple_of(((phase_y(p) * 2 + xl_) * 2 + core_) * (2 * HALF), 8)

    def copy_0(p, a):
        return pltpu.make_async_remote_copy(
            src_ref=wg.at[pl.ds(rows_of(p, a, 1 - core), 2 * HALF)], dst_ref=r0.at[p, a],
            send_sem=s0s.at[p, a], recv_sem=s0r.at[p, a], device_id=sibling, device_id_type=MESH,
        )

    def copy_x1(p, j):
        return pltpu.make_async_remote_copy(
            src_ref=qx1.at[p, j - 1], dst_ref=rx1.at[p, j - 1], send_sem=x1s.at[p, j - 1],
            recv_sem=x1r.at[p, j - 1], device_id=place(y, x_peer(j), core, z), device_id_type=MESH,
        )

    def copy_y1(p, a):
        return pltpu.make_async_remote_copy(
            src_ref=qy1.at[p, a], dst_ref=ry1.at[p, a], send_sem=y1s.at[p, a], recv_sem=y1r.at[p, a],
            device_id=place(phase_y(p), x, core, z), device_id_type=MESH,
        )

    def steps_to(h, a):
        return lax.rem(h * 2 + a - x + 4, 4)

    def send1(p, a):
        copy_0(p, a).wait_recv()
        pair[...] = wg[pl.ds(rows_of(p, a, core), 2 * HALF), :] + r0[p, a]
        for h in range(2):
            for k in range(8):
                parted[h, SHARE * k : SHARE * (k + 1), :] = pair[SHARE * (2 * k + h) : SHARE * (2 * k + h + 1), :]
        for h in range(2):
            j = steps_to(h, a)
            coded = encode(parted[h, :, 0:128])

            @pl.when(j != 0)
            def _():
                qx1[p, j - 1] = coded
                copy_x1(p, j).start()

            @pl.when(j == 0)
            def _():
                ownx[p] = parted[h, :, 0:128]

        for h in range(2):
            if p < 3:
                qy1[p, a, h] = encode(parted[h, :, 128:256])
            else:
                owny[a, h] = parted[h, :, 128:256]
        if p < 3:
            go(copy_y1(p, a))

    def copy_x2(p):
        return pltpu.make_async_remote_copy(
            src_ref=qx2.at[p], dst_ref=rx2.at[p], send_sem=x2s.at[p], recv_sem=x2r.at[p],
            device_id=place(phase_y(p), x, core, z), device_id_type=MESH,
        )

    def copy_y2(j):
        return pltpu.make_async_remote_copy(
            src_ref=qy2.at[j - 1], dst_ref=ry2.at[j - 1], send_sem=y2s.at[j - 1], recv_sem=y2r.at[j - 1],
            device_id=place(y, x_peer(j), core, z), device_id_type=MESH,
        )

    def send2x(p):
        v = ownx[p]
        for j in (1, 3, 2):
            copy_x1(p, j).wait_recv()
            v = v + decode(rx1[p, j - 1])
        if p < 3:
            qx2[p] = encode(v)
            go(copy_x2(p))
        else:
            total[0:HALF, 0:128] = v

    def send2y(a):
        for p in range(3):
            copy_y1(p, a).wait_recv()
        for h in range(2):
            j = steps_to(h, a)
            v = owny[a, h]
            for p in range(3):
                v = v + decode(ry1[p, a, h])
            coded = encode(v)

            @pl.when(j != 0)
            def _():
                qy2[j - 1] = coded
                copy_y2(j).start()

            @pl.when(j == 0)
            def _():
                total[0:HALF, 128:256] = v

    row32 = lax.broadcasted_iota(jnp.int32, (32, 256), 0)

    def copy_3(j):
        return pltpu.make_async_remote_copy(
            src_ref=q3.at[z_peer(j)], dst_ref=r3.at[j - 1], send_sem=s3s.at[j - 1], recv_sem=s3r.at[j - 1],
            device_id=place(y, x, core, z_peer(j)), device_id_type=MESH,
        )

    def send3():
        v = total[0:HALF, 0:128]
        for p in range(3):
            copy_x2(p).wait_recv()
            v = v + decode(rx2[p])
        total[0:HALF, 0:128] = v
        v = total[0:HALF, 128:256]
        for j in (1, 2, 3):
            copy_y2(j).wait_recv()
            v = v + decode(ry2[j - 1])
        total[0:HALF, 128:256] = v
        total[HALF:PADDED, :] = jnp.zeros((PADDED - HALF, 256), F32)
        for s in range(8):
            v = jnp.where(row32 < SHARE, total[SHARE * s : SHARE * s + 32, :], 0.0)
            k = exponent(v)
            q = jnp.floor(v * (jnp.exp2(-k) * UNIT) + 0.5)
            q3[s] = jnp.where(row32 < SHARE, q, k).astype(jnp.int32).astype(jnp.int16)
        for j in (4, 3, 5, 2, 6, 1, 7):
            go(copy_3(j))

    def finish():
        def value(q):
            w = q.astype(jnp.int32).astype(F32)
            return w * (jnp.exp2(w[31:32]) * (1.0 / UNIT))

        v = value(q3[z])
        for j in (1, 7, 2, 6, 3, 5, 4):
            copy_3(j).wait_recv()
            v = v + value(r3[j - 1])
        v = v * scale
        wg_ref[pl.ds(0, SHARE, stride=2), :] = v[:SHARE, 0:128]
        wg_ref[pl.ds(1, SHARE, stride=2), :] = v[:SHARE, 128:256]

    keep256 = jnp.where(z_of(256) < 8, 1.0, second)

    def convolve(fr, dst, transposed, lo, hi):
        def tile(t, _):
            acc = None
            for o in range(27):
                dx, dy, dz = o // 9, o // 3 % 3, o % 3
                a = fr[dz, pl.ds(2 * t + dx, 2), pl.ds(dy, 8)].reshape(256, 256)
                if transposed:
                    term = lax.dot_general(
                        a, w_all[26 - o], (((1,), (1,)), ((), ())), preferred_element_type=F32
                    )
                else:
                    term = jnp.dot(a, w_all[o], preferred_element_type=F32)
                acc = term if acc is None else acc + term
            dst[pl.ds(2 * t, 2)] = (acc * keep256).astype(BF16).reshape(2, 8, 16, 256)
            return 0

        lax.fori_loop(lo, hi, tile, 0)

    done = 0
    for n, (p, a) in enumerate(PHASES):
        for i in range(done, ENDS[n]):
            gradient(i)
        done = ENDS[n]
        copy_0(p, a).start()
        if n >= 2:
            send1(*PHASES[n - 2])
    send1(*PHASES[6])
    loads[2].wait()
    convolve(g_fr, ig_ref, True, 0, 1)
    send1(*PHASES[7])
    convolve(g_fr, ig_ref, True, 1, 4)
    send2x(0)
    send2x(1)
    send2y(0)
    send2y(1)
    send2x(2)
    send2x(3)
    send3()
    near_columns(2, f_halo, f_fr)
    convolve(f_fr, out_ref, False, 0, 4)
    finish()
    for c in started:
        c.wait_send()
    for p, a in PHASES:
        copy_0(p, a).wait_send()
    for j in (1, 2, 3):
        for p in range(4):
            copy_x1(p, j).wait_send()
        copy_y2(j).wait_send()


def hand_over(a, b, c, a_out, b_out, c_out, a_buf, b_buf, c_buf, in_sems, out_sems):
    moves = [(a, a_buf, a_out, pl.ds(2 * i, 2)) for i in range(4)]
    moves += [(b, b_buf, b_out, pl.ds(2 * i, 2)) for i in range(4)]
    moves += [(c, c_buf, c_out, pl.ds(0, 2 * SHARE))]
    ins = [pltpu.make_async_copy(v.at[part], buf.at[part], in_sems.at[i]) for i, (v, buf, _, part) in enumerate(moves)]
    outs = [pltpu.make_async_copy(buf.at[part], o.at[part], out_sems.at[i]) for i, (_, buf, o, part) in enumerate(moves)]
    for copy in ins:
        copy.start()
    for copy_in, copy_out in zip(ins, outs):
        copy_in.wait()
        copy_out.start()
    for copy in outs:
        copy.wait()


def per_device(features, cotangent, weights, levels, counts):
    f = features.reshape(8, 8, 16, 256)
    g = cotangent.reshape(8, 8, 16, 256)
    scale = 1.0 / math.sqrt(1024 * lax.axis_size("gx") * lax.axis_size("gy"))
    vmem = pl.BlockSpec(memory_space=pltpu.VMEM)
    smem = pl.BlockSpec(memory_space=pltpu.SMEM)
    anywhere = pl.BlockSpec(memory_space=pl.ANY)
    dma = pltpu.SemaphoreType.DMA
    i16 = jnp.int16
    out, ig, wgrad = pl.pallas_call(
        functools.partial(kernel, scale),
        out_shape=(
            jax.ShapeDtypeStruct((8, 8, 16, 256), BF16),
            jax.ShapeDtypeStruct((8, 8, 16, 256), BF16),
            jax.ShapeDtypeStruct((2 * SHARE, 128), F32),
        ),
        in_specs=[smem, smem, anywhere, anywhere, anywhere],
        out_specs=(vmem, vmem, vmem),
        scratch_shapes=[
            pltpu.VMEM((8, 8, 16, 256), BF16),
            pltpu.VMEM((8, 8, 16, 256), BF16),
            pltpu.VMEM((27, 256, 256), BF16),
            pltpu.VMEM((3, 10, 10, 16, 256), BF16),
            pltpu.VMEM((3, 10, 10, 16, 256), BF16),
            pltpu.VMEM((36, 16, 256), BF16),
            pltpu.VMEM((36, 16, 256), BF16),
            pltpu.VMEM((8, 256), F32),
            pltpu.VMEM((8, 8, 256), F32),
            pltpu.VMEM((256, 1024), BF16),
            pltpu.VMEM((6912, 256), F32),
            pltpu.VMEM((4, 2, 2 * HALF, 256), F32),
            pltpu.VMEM((2 * HALF, 256), F32),
            pltpu.VMEM((2, HALF, 256), F32),
            pltpu.VMEM((4, 3, PADDED, 128), i16),
            pltpu.VMEM((3, 2, 2, PADDED, 128), i16),
            pltpu.VMEM((4, HALF, 128), F32),
            pltpu.VMEM((2, 2, HALF, 128), F32),
            pltpu.VMEM((4, 3, PADDED, 128), i16),
            pltpu.VMEM((3, 2, 2, PADDED, 128), i16),
            pltpu.VMEM((3, PADDED, 128), i16),
            pltpu.VMEM((3, PADDED, 128), i16),
            pltpu.VMEM((3, PADDED, 128), i16),
            pltpu.VMEM((3, PADDED, 128), i16),
            pltpu.VMEM((PADDED, 256), F32),
            pltpu.VMEM((8, 32, 256), i16),
            pltpu.VMEM((7, 32, 256), i16),
            dma((3,)),
            dma((3, 8)),
            dma((3, 8)),
            dma((4, 2)),
            dma((4, 2)),
            dma((4, 3)),
            dma((4, 3)),
            dma((3, 2)),
            dma((3, 2)),
            dma((3,)),
            dma((3,)),
            dma((3,)),
            dma((3,)),
            dma((7,)),
            dma((7,)),
        ],
        compiler_params=pltpu.CompilerParams(
            collective_id=0, has_side_effects=True, vmem_limit_bytes=56 * 1024 * 1024
        ),
    )(levels, counts, f, g, weights)
    out, ig, wgrad = pl.pallas_call(
        hand_over,
        out_shape=tuple(jax.ShapeDtypeStruct(v.shape, v.dtype) for v in (out, ig, wgrad)),
        in_specs=[anywhere] * 3,
        out_specs=(anywhere,) * 3,
        scratch_shapes=[
            pltpu.VMEM(out.shape, BF16),
            pltpu.VMEM(ig.shape, BF16),
            pltpu.VMEM(wgrad.shape, F32),
            dma((9,)),
            dma((9,)),
        ],
    )(out, ig, wgrad)
    shape = features.shape
    return out.reshape(shape), ig.reshape(shape), wgrad.reshape(-1)


def solution(mesh):
    return jax.shard_map(
        per_device,
        mesh=mesh,
        in_specs=(
            P("gx", "gy", None, None, None),
            P("gx", "gy", None, None, None),
            P(),
            P("gx", "gy", None),
            P("gx", "gy"),
        ),
        out_specs=(
            P("gx", "gy", None, None, None),
            P("gx", "gy", None, None, None),
            P(("gx", "gy")),
        ),
        check_vma=False,
    )
```

```python
import functools
import math

import jax
import jax.numpy as jnp
from jax import lax
from jax.experimental import pallas as pl
from jax.experimental.pallas import tpu as pltpu
from jax.sharding import PartitionSpec as P

F32 = jnp.float32
BF16 = jnp.bfloat16
MESH = pl.DeviceIdType.MESH

DIRS = ((-1, 0), (1, 0), (0, -1), (0, 1), (-1, -1), (-1, 1), (1, -1), (1, 1))
COLS = (0, 8, 16, 24, 32, 33, 34, 35)
WIDE = (8, 8, 8, 8, 1, 1, 1, 1)
PHASES = tuple((p, a) for p in range(4) for a in range(2))
ENDS = (5, 8, 11, 15, 18, 21, 25, 27)
SHARE = 27
HALF = 8 * SHARE
PADDED = 224
UNIT = 32000.0


def up_down(v, top, bottom, z):
    rows = v.shape[0]
    lower = jnp.where(z == 0, bottom, pltpu.roll(v, 1, 0))
    higher = jnp.where(z == 15, top, pltpu.roll(v, rows - 1, 0))
    return lower, higher


def exponent(v):
    peak = jnp.max(jnp.abs(v), axis=0, keepdims=True)
    return jnp.ceil(jnp.log2(jnp.maximum(peak, 1e-30)))


def encode(v):
    k = exponent(v)
    q = jnp.floor(v * (jnp.exp2(-k) * UNIT) + 0.5)
    tail = jnp.broadcast_to(k, (PADDED - HALF, v.shape[1]))
    return jnp.concatenate([q, tail], axis=0).astype(jnp.int32).astype(jnp.int16)


def decode(q):
    w = q.astype(jnp.int32).astype(F32)
    return w[:HALF] * (jnp.exp2(w[HALF : HALF + 1]) * (1.0 / UNIT))


def kernel(
    scale, lev, cnt, f_hbm, g_hbm, w_hbm, out_ref, ig_ref, wg_ref,
    f_own, g_own, w_all, f_fr, g_fr, f_halo, g_halo, meta, near, ft, wg,
    r0, pair, parted, qx1, qy1, ownx, owny, rx1, ry1, qx2, qy2, rx2, ry2, total, q3, r3,
    load_sem, hs, hr, s0s, s0r, x1s, x1r, y1s, y1r, x2s, x2r, y2s, y2r, s3s, s3r,
):
    gx, gy = lax.axis_index("gx"), lax.axis_index("gy")
    y, xl, core = lax.div(gx, 4), lax.rem(lax.div(gx, 2), 2), lax.rem(gx, 2)
    z, xh = lax.div(gy, 2), lax.rem(gy, 2)
    x = xh * 2 + xl

    def place(y_, x_, core_, z_):
        return (y_ * 4 + lax.rem(x_, 2) * 2 + core_, z_ * 2 + lax.div(x_, 2))

    sibling = place(y, x, 1 - core, z)

    def x_peer(j):
        return lax.rem(x + j, 4)

    def y_peer(j):
        return lax.rem(y + j, 4)

    def z_peer(j):
        return lax.rem(z + j, 8)

    def neighbour(d):
        return (lax.rem(gx + d[0] + 16, 16), lax.rem(gy + d[1] + 16, 16))

    loads = [
        pltpu.make_async_copy(g_hbm, g_own, load_sem.at[0]),
        pltpu.make_async_copy(f_hbm, f_own, load_sem.at[1]),
        pltpu.make_async_copy(w_hbm, w_all, load_sem.at[2]),
    ]
    for c in loads:
        c.start()

    barrier = pltpu.get_barrier_semaphore()
    for d in DIRS:
        pl.semaphore_signal(barrier, inc=1, device_id=neighbour(d), device_id_type=MESH)
    pl.semaphore_signal(barrier, inc=1, device_id=sibling, device_id_type=MESH)
    for j in (1, 2, 3):
        pl.semaphore_signal(barrier, inc=1, device_id=place(y, x_peer(j), core, z), device_id_type=MESH)
        pl.semaphore_signal(barrier, inc=1, device_id=place(y_peer(j), x, core, z), device_id_type=MESH)
    for j in range(1, 8):
        pl.semaphore_signal(barrier, inc=1, device_id=place(y, x, core, z_peer(j)), device_id_type=MESH)

    shift = lev[0, 0, 0].astype(F32)
    second = jnp.where(cnt[0, 0] >= 2, 1.0, 0.0).astype(F32)
    eight = lax.broadcasted_iota(jnp.int32, (8, 256), 0)
    meta[...] = jnp.where(eight < 4, shift, second)
    loads[0].wait()
    loads[1].wait()
    pl.semaphore_wait(barrier, 22)

    def edge(ref, d):
        row = {-1: 0, 1: 7}
        if d[0] and d[1]:
            return ref.at[row[d[0]], row[d[1]]]
        return ref.at[row[d[0]]] if d[0] else ref.at[:, row[d[1]]]

    def slot(ref, i):
        return ref.at[COLS[i]] if WIDE[i] == 1 else ref.at[pl.ds(COLS[i], 8)]

    def halo(kind, i):
        d = DIRS[i]
        opposite = DIRS.index((-d[0], -d[1]))
        if kind == 0:
            src, dst = meta, near.at[opposite]
        else:
            src = edge((None, g_own, f_own)[kind], d)
            dst = slot((None, g_halo, f_halo)[kind], opposite)
        return pltpu.make_async_remote_copy(
            src_ref=src, dst_ref=dst, send_sem=hs.at[kind, i], recv_sem=hr.at[kind, opposite],
            device_id=neighbour(d), device_id_type=MESH,
        )

    started = []

    def go(copy):
        copy.start()
        started.append(copy)

    for i in (4, 5, 6, 7, 2, 3, 0, 1):
        go(halo(0, i))
        go(halo(1, i))

    def z_of(rows):
        return lax.rem(lax.broadcasted_iota(jnp.int32, (rows, 256), 0), 16)

    z128 = z_of(128)
    keep128 = jnp.where(z128 < 8, 1.0, second)

    def own_columns(src, fr, with_transpose):
        for r in range(8):
            v = src[r].reshape(128, 256).astype(F32) * keep128
            lower, higher = up_down(v, 0.0, 0.0, z128)
            for k, t in enumerate((lower, v, higher)):
                fr[k, r + 1, 1:9] = t.astype(BF16).reshape(8, 16, 256)
            if with_transpose:
                ft[:, r * 128 : (r + 1) * 128] = v.T.astype(BF16)

    own_columns(g_own, g_fr, False)
    own_columns(f_own, f_fr, True)

    def near_columns(kind, recv, fr):
        for i, (dx, dy) in enumerate(DIRS):
            if kind == 1:
                halo(0, DIRS.index((-dx, -dy))).wait_recv()
            halo(kind, DIRS.index((-dx, -dy))).wait_recv()
            n = WIDE[i]
            inside = jnp.logical_and(
                jnp.logical_and(gx + dx >= 0, gx + dx < 16), jnp.logical_and(gy + dy >= 0, gy + dy < 16)
            )
            valid = jnp.where(inside, 1.0, 0.0).astype(F32)
            higher_by = near[i, 0:1, :] - shift
            level = jnp.where(higher_by == 0.0, valid, 0.0)
            above = jnp.where(higher_by == 1.0, valid, 0.0)
            below = jnp.where(higher_by == -1.0, valid, 0.0)
            rows = n * 16
            zr = z_of(rows)
            v = recv[COLS[i] : COLS[i] + n].reshape(rows, 256).astype(F32)
            v = v * jnp.where(zr < 8, 1.0, near[i, 4:5, :])
            swapped = pltpu.roll(v, 8, 0) if n == 1 else None
            up8 = swapped if n == 1 else pltpu.roll(v, 8, 0)
            down8 = swapped if n == 1 else pltpu.roll(v, rows - 8, 0)
            c = level * v + jnp.where(zr >= 8, above * up8, below * down8)
            top = above * pltpu.roll(v, 7, 0)
            bottom = below * pltpu.roll(v, rows - 7, 0)
            lower, higher = up_down(c, top, bottom, zr)
            xs = {-1: 0, 0: slice(1, 9), 1: 9}[dx]
            ys = {-1: 0, 0: slice(1, 9), 1: 9}[dy]
            for k, t in enumerate((lower, c, higher)):
                t = t.astype(BF16)
                fr[k, xs, ys] = t if n == 1 else t.reshape(8, 16, 256)

    near_columns(1, g_halo, g_fr)
    for i in range(8):
        go(halo(2, i))

    first = y_peer(1)
    base = lax.div(27 * first, 4)

    def gradient(i):
        o = lax.rem(base + i, 27)
        dx, dy, dz = lax.div(o, 9), lax.rem(lax.div(o, 3), 3), lax.rem(o, 3)
        g = g_fr[2 - dz, pl.ds(2 - dx, 8), pl.ds(2 - dy, 8)].reshape(1024, 256)
        wg[pl.ds(pl.multiple_of(o * 256, 256), 256), :] = jnp.dot(ft[...], g, preferred_element_type=F32)

    def phase_y(p):
        return lax.rem(y + 1 + p, 4)

    def rows_of(p, xl_, core_):
        return pl.multiple_of(((phase_y(p) * 2 + xl_) * 2 + core_) * (2 * HALF), 8)

    def copy_0(p, a):
        return pltpu.make_async_remote_copy(
            src_ref=wg.at[pl.ds(rows_of(p, a, 1 - core), 2 * HALF)], dst_ref=r0.at[p, a],
            send_sem=s0s.at[p, a], recv_sem=s0r.at[p, a], device_id=sibling, device_id_type=MESH,
        )

    def copy_x1(p, j):
        return pltpu.make_async_remote_copy(
            src_ref=qx1.at[p, j - 1], dst_ref=rx1.at[p, j - 1], send_sem=x1s.at[p, j - 1],
            recv_sem=x1r.at[p, j - 1], device_id=place(y, x_peer(j), core, z), device_id_type=MESH,
        )

    def copy_y1(p, a):
        return pltpu.make_async_remote_copy(
            src_ref=qy1.at[p, a], dst_ref=ry1.at[p, a], send_sem=y1s.at[p, a], recv_sem=y1r.at[p, a],
            device_id=place(phase_y(p), x, core, z), device_id_type=MESH,
        )

    def steps_to(h, a):
        return lax.rem(h * 2 + a - x + 4, 4)

    def send1(p, a):
        copy_0(p, a).wait_recv()
        pair[...] = wg[pl.ds(rows_of(p, a, core), 2 * HALF), :] + r0[p, a]
        for h in range(2):
            for k in range(8):
                parted[h, SHARE * k : SHARE * (k + 1), :] = pair[SHARE * (2 * k + h) : SHARE * (2 * k + h + 1), :]
        for h in range(2):
            j = steps_to(h, a)
            coded = encode(parted[h, :, 0:128])

            @pl.when(j != 0)
            def _():
                qx1[p, j - 1] = coded
                copy_x1(p, j).start()

            @pl.when(j == 0)
            def _():
                ownx[p] = parted[h, :, 0:128]

        for h in range(2):
            if p < 3:
                qy1[p, a, h] = encode(parted[h, :, 128:256])
            else:
                owny[a, h] = parted[h, :, 128:256]
        if p < 3:
            go(copy_y1(p, a))

    def copy_x2(p):
        return pltpu.make_async_remote_copy(
            src_ref=qx2.at[p], dst_ref=rx2.at[p], send_sem=x2s.at[p], recv_sem=x2r.at[p],
            device_id=place(phase_y(p), x, core, z), device_id_type=MESH,
        )

    def copy_y2(j):
        return pltpu.make_async_remote_copy(
            src_ref=qy2.at[j - 1], dst_ref=ry2.at[j - 1], send_sem=y2s.at[j - 1], recv_sem=y2r.at[j - 1],
            device_id=place(y, x_peer(j), core, z), device_id_type=MESH,
        )

    def send2x(p):
        v = ownx[p]
        for j in (1, 3, 2):
            copy_x1(p, j).wait_recv()
            v = v + decode(rx1[p, j - 1])
        if p < 3:
            qx2[p] = encode(v)
            go(copy_x2(p))
        else:
            total[0:HALF, 0:128] = v

    def send2y(a):
        for p in range(3):
            copy_y1(p, a).wait_recv()
        for h in range(2):
            j = steps_to(h, a)
            v = owny[a, h]
            for p in range(3):
                v = v + decode(ry1[p, a, h])
            coded = encode(v)

            @pl.when(j != 0)
            def _():
                qy2[j - 1] = coded
                copy_y2(j).start()

            @pl.when(j == 0)
            def _():
                total[0:HALF, 128:256] = v

    row32 = lax.broadcasted_iota(jnp.int32, (32, 256), 0)

    def copy_3(j):
        return pltpu.make_async_remote_copy(
            src_ref=q3.at[z_peer(j)], dst_ref=r3.at[j - 1], send_sem=s3s.at[j - 1], recv_sem=s3r.at[j - 1],
            device_id=place(y, x, core, z_peer(j)), device_id_type=MESH,
        )

    def send3():
        v = total[0:HALF, 0:128]
        for p in range(3):
            copy_x2(p).wait_recv()
            v = v + decode(rx2[p])
        total[0:HALF, 0:128] = v
        v = total[0:HALF, 128:256]
        for j in (1, 2, 3):
            copy_y2(j).wait_recv()
            v = v + decode(ry2[j - 1])
        total[0:HALF, 128:256] = v
        total[HALF:PADDED, :] = jnp.zeros((PADDED - HALF, 256), F32)
        for s in range(8):
            v = jnp.where(row32 < SHARE, total[SHARE * s : SHARE * s + 32, :], 0.0)
            k = exponent(v)
            q = jnp.floor(v * (jnp.exp2(-k) * UNIT) + 0.5)
            q3[s] = jnp.where(row32 < SHARE, q, k).astype(jnp.int32).astype(jnp.int16)
        for j in (4, 3, 5, 2, 6, 1, 7):
            go(copy_3(j))

    def finish():
        def value(q):
            w = q.astype(jnp.int32).astype(F32)
            return w * (jnp.exp2(w[31:32]) * (1.0 / UNIT))

        v = value(q3[z])
        for j in (1, 7, 2, 6, 3, 5, 4):
            copy_3(j).wait_recv()
            v = v + value(r3[j - 1])
        v = v * scale
        wg_ref[pl.ds(0, SHARE, stride=2), :] = v[:SHARE, 0:128]
        wg_ref[pl.ds(1, SHARE, stride=2), :] = v[:SHARE, 128:256]

    keep256 = jnp.where(z_of(256) < 8, 1.0, second)

    def convolve(fr, dst, transposed, lo, hi):
        def tile(t, _):
            acc = None
            for o in range(27):
                dx, dy, dz = o // 9, o // 3 % 3, o % 3
                a = fr[dz, pl.ds(2 * t + dx, 2), pl.ds(dy, 8)].reshape(256, 256)
                if transposed:
                    term = lax.dot_general(
                        a, w_all[26 - o], (((1,), (1,)), ((), ())), preferred_element_type=F32
                    )
                else:
                    term = jnp.dot(a, w_all[o], preferred_element_type=F32)
                acc = term if acc is None else acc + term
            dst[pl.ds(2 * t, 2)] = (acc * keep256).astype(BF16).reshape(2, 8, 16, 256)
            return 0

        lax.fori_loop(lo, hi, tile, 0)

    done = 0
    for n, (p, a) in enumerate(PHASES):
        for i in range(done, ENDS[n]):
            gradient(i)
        done = ENDS[n]
        copy_0(p, a).start()
        if n >= 2:
            send1(*PHASES[n - 2])
    send1(*PHASES[6])
    send1(*PHASES[7])
    loads[2].wait()
    convolve(g_fr, ig_ref, True, 0, 4)
    send2x(0)
    send2x(1)
    near_columns(2, f_halo, f_fr)
    convolve(f_fr, out_ref, False, 0, 1)
    send2y(0)
    send2y(1)
    send2x(2)
    send2x(3)
    send3()
    convolve(f_fr, out_ref, False, 1, 4)
    finish()
    for c in started:
        c.wait_send()
    for p, a in PHASES:
        copy_0(p, a).wait_send()
    for j in (1, 2, 3):
        for p in range(4):
            copy_x1(p, j).wait_send()
        copy_y2(j).wait_send()


def hand_over(a, b, c, a_out, b_out, c_out, a_buf, b_buf, c_buf, in_sems, out_sems):
    moves = [(a, a_buf, a_out, pl.ds(2 * i, 2)) for i in range(4)]
    moves += [(b, b_buf, b_out, pl.ds(2 * i, 2)) for i in range(4)]
    moves += [(c, c_buf, c_out, pl.ds(0, 2 * SHARE))]
    ins = [pltpu.make_async_copy(v.at[part], buf.at[part], in_sems.at[i]) for i, (v, buf, _, part) in enumerate(moves)]
    outs = [pltpu.make_async_copy(buf.at[part], o.at[part], out_sems.at[i]) for i, (_, buf, o, part) in enumerate(moves)]
    for copy in ins:
        copy.start()
    for copy_in, copy_out in zip(ins, outs):
        copy_in.wait()
        copy_out.start()
    for copy in outs:
        copy.wait()


def per_device(features, cotangent, weights, levels, counts):
    f = features.reshape(8, 8, 16, 256)
    g = cotangent.reshape(8, 8, 16, 256)
    scale = 1.0 / math.sqrt(1024 * lax.axis_size("gx") * lax.axis_size("gy"))
    vmem = pl.BlockSpec(memory_space=pltpu.VMEM)
    smem = pl.BlockSpec(memory_space=pltpu.SMEM)
    anywhere = pl.BlockSpec(memory_space=pl.ANY)
    dma = pltpu.SemaphoreType.DMA
    i16 = jnp.int16
    out, ig, wgrad = pl.pallas_call(
        functools.partial(kernel, scale),
        out_shape=(
            jax.ShapeDtypeStruct((8, 8, 16, 256), BF16),
            jax.ShapeDtypeStruct((8, 8, 16, 256), BF16),
            jax.ShapeDtypeStruct((2 * SHARE, 128), F32),
        ),
        in_specs=[smem, smem, anywhere, anywhere, anywhere],
        out_specs=(vmem, vmem, vmem),
        scratch_shapes=[
            pltpu.VMEM((8, 8, 16, 256), BF16),
            pltpu.VMEM((8, 8, 16, 256), BF16),
            pltpu.VMEM((27, 256, 256), BF16),
            pltpu.VMEM((3, 10, 10, 16, 256), BF16),
            pltpu.VMEM((3, 10, 10, 16, 256), BF16),
            pltpu.VMEM((36, 16, 256), BF16),
            pltpu.VMEM((36, 16, 256), BF16),
            pltpu.VMEM((8, 256), F32),
            pltpu.VMEM((8, 8, 256), F32),
            pltpu.VMEM((256, 1024), BF16),
            pltpu.VMEM((6912, 256), F32),
            pltpu.VMEM((4, 2, 2 * HALF, 256), F32),
            pltpu.VMEM((2 * HALF, 256), F32),
            pltpu.VMEM((2, HALF, 256), F32),
            pltpu.VMEM((4, 3, PADDED, 128), i16),
            pltpu.VMEM((3, 2, 2, PADDED, 128), i16),
            pltpu.VMEM((4, HALF, 128), F32),
            pltpu.VMEM((2, 2, HALF, 128), F32),
            pltpu.VMEM((4, 3, PADDED, 128), i16),
            pltpu.VMEM((3, 2, 2, PADDED, 128), i16),
            pltpu.VMEM((3, PADDED, 128), i16),
            pltpu.VMEM((3, PADDED, 128), i16),
            pltpu.VMEM((3, PADDED, 128), i16),
            pltpu.VMEM((3, PADDED, 128), i16),
            pltpu.VMEM((PADDED, 256), F32),
            pltpu.VMEM((8, 32, 256), i16),
            pltpu.VMEM((7, 32, 256), i16),
            dma((3,)),
            dma((3, 8)),
            dma((3, 8)),
            dma((4, 2)),
            dma((4, 2)),
            dma((4, 3)),
            dma((4, 3)),
            dma((3, 2)),
            dma((3, 2)),
            dma((3,)),
            dma((3,)),
            dma((3,)),
            dma((3,)),
            dma((7,)),
            dma((7,)),
        ],
        compiler_params=pltpu.CompilerParams(
            collective_id=0, has_side_effects=True, vmem_limit_bytes=56 * 1024 * 1024
        ),
    )(levels, counts, f, g, weights)
    out, ig, wgrad = pl.pallas_call(
        hand_over,
        out_shape=tuple(jax.ShapeDtypeStruct(v.shape, v.dtype) for v in (out, ig, wgrad)),
        in_specs=[anywhere] * 3,
        out_specs=(anywhere,) * 3,
        scratch_shapes=[
            pltpu.VMEM(out.shape, BF16),
            pltpu.VMEM(ig.shape, BF16),
            pltpu.VMEM(wgrad.shape, F32),
            dma((9,)),
            dma((9,)),
        ],
    )(out, ig, wgrad)
    shape = features.shape
    return out.reshape(shape), ig.reshape(shape), wgrad.reshape(-1)


def solution(mesh):
    return jax.shard_map(
        per_device,
        mesh=mesh,
        in_specs=(
            P("gx", "gy", None, None, None),
            P("gx", "gy", None, None, None),
            P(),
            P("gx", "gy", None),
            P("gx", "gy"),
        ),
        out_specs=(
            P("gx", "gy", None, None, None),
            P("gx", "gy", None, None, None),
            P(("gx", "gy")),
        ),
        check_vma=False,
    )
```

```python
import functools
import math

import jax
import jax.numpy as jnp
from jax import lax
from jax.experimental import pallas as pl
from jax.experimental.pallas import tpu as pltpu
from jax.sharding import PartitionSpec as P

F32 = jnp.float32
BF16 = jnp.bfloat16
MESH = pl.DeviceIdType.MESH

DIRS = ((-1, 0), (1, 0), (0, -1), (0, 1), (-1, -1), (-1, 1), (1, -1), (1, 1))
COLS = (0, 8, 16, 24, 32, 33, 34, 35)
WIDE = (8, 8, 8, 8, 1, 1, 1, 1)
PHASES = tuple((p, a) for p in range(4) for a in range(2))
ENDS = (5, 8, 11, 15, 18, 21, 25, 27)
SHARE = 27
HALF = 8 * SHARE
PADDED = 224
UNIT = 32000.0


def up_down(v, top, bottom, z):
    rows = v.shape[0]
    lower = jnp.where(z == 0, bottom, pltpu.roll(v, 1, 0))
    higher = jnp.where(z == 15, top, pltpu.roll(v, rows - 1, 0))
    return lower, higher


def exponent(v):
    peak = jnp.max(jnp.abs(v), axis=0, keepdims=True)
    return jnp.ceil(jnp.log2(jnp.maximum(peak, 1e-30)))


def encode(v):
    k = exponent(v)
    q = jnp.floor(v * (jnp.exp2(-k) * UNIT) + 0.5)
    tail = jnp.broadcast_to(k, (PADDED - HALF, v.shape[1]))
    return jnp.concatenate([q, tail], axis=0).astype(jnp.int32).astype(jnp.int16)


def decode(q):
    w = q.astype(jnp.int32).astype(F32)
    return w[:HALF] * (jnp.exp2(w[HALF : HALF + 1]) * (1.0 / UNIT))


def kernel(
    scale, lev_hbm, cnt_hbm, f_hbm, g_hbm, w_hbm, out_hbm, ig_hbm, wg_hbm,
    lev, cnt, out_ref, ig_ref, wg_ref,
    f_own, g_own, w_all, f_fr, g_fr, f_halo, g_halo, meta, near, ft, wg,
    r0, pair, parted, qx1, qy1, ownx, owny, rx1, ry1, qx2, qy2, rx2, ry2, total, q3, r3,
    load_sem, store_sem, hs, hr, s0s, s0r, x1s, x1r, y1s, y1r, x2s, x2r, y2s, y2r, s3s, s3r,
):
    gx, gy = lax.axis_index("gx"), lax.axis_index("gy")
    y, xl, core = lax.div(gx, 4), lax.rem(lax.div(gx, 2), 2), lax.rem(gx, 2)
    z, xh = lax.div(gy, 2), lax.rem(gy, 2)
    x = xh * 2 + xl

    def place(y_, x_, core_, z_):
        return (y_ * 4 + lax.rem(x_, 2) * 2 + core_, z_ * 2 + lax.div(x_, 2))

    sibling = place(y, x, 1 - core, z)

    def x_peer(j):
        return lax.rem(x + j, 4)

    def y_peer(j):
        return lax.rem(y + j, 4)

    def z_peer(j):
        return lax.rem(z + j, 8)

    def neighbour(d):
        return (lax.rem(gx + d[0] + 16, 16), lax.rem(gy + d[1] + 16, 16))

    loads = [
        pltpu.make_async_copy(g_hbm, g_own, load_sem.at[0]),
        pltpu.make_async_copy(f_hbm, f_own, load_sem.at[1]),
        pltpu.make_async_copy(w_hbm, w_all, load_sem.at[2]),
        pltpu.make_async_copy(lev_hbm, lev, load_sem.at[3]),
        pltpu.make_async_copy(cnt_hbm, cnt, load_sem.at[4]),
    ]

    barrier = pltpu.get_barrier_semaphore()
    def greet(device):
        pl.semaphore_signal(barrier, inc=1, device_id=device, device_id_type=MESH)

    greet(place(y, x, core, z_peer(4)))
    for i in (4, 5, 6, 7):
        greet(neighbour(DIRS[i]))
    for i in (2, 3):
        greet(neighbour(DIRS[i]))
    for j in (3, 5, 2, 6):
        greet(place(y, x, core, z_peer(j)))
    for j in (2, 1, 3):
        greet(place(y, x_peer(j), core, z))
        greet(place(y_peer(j), x, core, z))
    for j in (1, 7):
        greet(place(y, x, core, z_peer(j)))
    for i in (0, 1):
        greet(neighbour(DIRS[i]))
    greet(sibling)
    for n in (3, 4, 0, 1, 2):
        loads[n].start()
    loads[3].wait()
    loads[4].wait()

    shift = lev[0, 0, 0].astype(F32)
    second = jnp.where(cnt[0, 0] >= 2, 1.0, 0.0).astype(F32)
    eight = lax.broadcasted_iota(jnp.int32, (8, 256), 0)
    meta[...] = jnp.where(eight < 4, shift, second)
    loads[0].wait()
    loads[1].wait()
    pl.semaphore_wait(barrier, 22)

    def edge(ref, d):
        row = {-1: 0, 1: 7}
        if d[0] and d[1]:
            return ref.at[row[d[0]], row[d[1]]]
        return ref.at[row[d[0]]] if d[0] else ref.at[:, row[d[1]]]

    def slot(ref, i):
        return ref.at[COLS[i]] if WIDE[i] == 1 else ref.at[pl.ds(COLS[i], 8)]

    def halo(kind, i):
        d = DIRS[i]
        opposite = DIRS.index((-d[0], -d[1]))
        if kind == 0:
            src, dst = meta, near.at[opposite]
        else:
            src = edge((None, g_own, f_own)[kind], d)
            dst = slot((None, g_halo, f_halo)[kind], opposite)
        return pltpu.make_async_remote_copy(
            src_ref=src, dst_ref=dst, send_sem=hs.at[kind, i], recv_sem=hr.at[kind, opposite],
            device_id=neighbour(d), device_id_type=MESH,
        )

    started = []

    def go(copy):
        copy.start()
        started.append(copy)

    for i in (4, 5, 6, 7, 2, 3, 0, 1):
        go(halo(0, i))
        go(halo(1, i))

    def z_of(rows):
        return lax.rem(lax.broadcasted_iota(jnp.int32, (rows, 256), 0), 16)

    z128 = z_of(128)
    keep128 = jnp.where(z128 < 8, 1.0, second)

    def own_columns(src, fr, with_transpose):
        for r in range(8):
            v = src[r].reshape(128, 256).astype(F32) * keep128
            lower, higher = up_down(v, 0.0, 0.0, z128)
            for k, t in enumerate((lower, v, higher)):
                fr[k, r + 1, 1:9] = t.astype(BF16).reshape(8, 16, 256)
            if with_transpose:
                ft[:, r * 128 : (r + 1) * 128] = v.T.astype(BF16)

    own_columns(g_own, g_fr, False)
    own_columns(f_own, f_fr, True)

    def near_columns(kind, recv, fr):
        for i in (0, 1, 4, 5, 6, 7, 2, 3):
            dx, dy = DIRS[i]
            if kind == 1:
                halo(0, DIRS.index((-dx, -dy))).wait_recv()
            halo(kind, DIRS.index((-dx, -dy))).wait_recv()
            n = WIDE[i]
            inside = jnp.logical_and(
                jnp.logical_and(gx + dx >= 0, gx + dx < 16), jnp.logical_and(gy + dy >= 0, gy + dy < 16)
            )
            valid = jnp.where(inside, 1.0, 0.0).astype(F32)
            higher_by = near[i, 0:1, :] - shift
            level = jnp.where(higher_by == 0.0, valid, 0.0)
            above = jnp.where(higher_by == 1.0, valid, 0.0)
            below = jnp.where(higher_by == -1.0, valid, 0.0)
            rows = n * 16
            zr = z_of(rows)
            v = recv[COLS[i] : COLS[i] + n].reshape(rows, 256).astype(F32)
            v = v * jnp.where(zr < 8, 1.0, near[i, 4:5, :])
            swapped = pltpu.roll(v, 8, 0) if n == 1 else None
            up8 = swapped if n == 1 else pltpu.roll(v, 8, 0)
            down8 = swapped if n == 1 else pltpu.roll(v, rows - 8, 0)
            c = level * v + jnp.where(zr >= 8, above * up8, below * down8)
            top = above * pltpu.roll(v, 7, 0)
            bottom = below * pltpu.roll(v, rows - 7, 0)
            lower, higher = up_down(c, top, bottom, zr)
            xs = {-1: 0, 0: slice(1, 9), 1: 9}[dx]
            ys = {-1: 0, 0: slice(1, 9), 1: 9}[dy]
            for k, t in enumerate((lower, c, higher)):
                t = t.astype(BF16)
                fr[k, xs, ys] = t if n == 1 else t.reshape(8, 16, 256)

    near_columns(1, g_halo, g_fr)
    for i in range(8):
        go(halo(2, i))

    first = y_peer(1)
    base = lax.div(27 * first, 4)

    def gradient(i):
        o = lax.rem(base + i, 27)
        dx, dy, dz = lax.div(o, 9), lax.rem(lax.div(o, 3), 3), lax.rem(o, 3)
        g = g_fr[2 - dz, pl.ds(2 - dx, 8), pl.ds(2 - dy, 8)].reshape(1024, 256)
        wg[pl.ds(pl.multiple_of(o * 256, 256), 256), :] = jnp.dot(ft[...], g, preferred_element_type=F32)

    def phase_y(p):
        return lax.rem(y + 1 + p, 4)

    def rows_of(p, xl_, core_):
        return pl.multiple_of(((phase_y(p) * 2 + xl_) * 2 + core_) * (2 * HALF), 8)

    def copy_0(p, a):
        return pltpu.make_async_remote_copy(
            src_ref=wg.at[pl.ds(rows_of(p, a, 1 - core), 2 * HALF)], dst_ref=r0.at[p, a],
            send_sem=s0s.at[p, a], recv_sem=s0r.at[p, a], device_id=sibling, device_id_type=MESH,
        )

    def copy_x1(p, j):
        return pltpu.make_async_remote_copy(
            src_ref=qx1.at[p, j - 1], dst_ref=rx1.at[p, j - 1], send_sem=x1s.at[p, j - 1],
            recv_sem=x1r.at[p, j - 1], device_id=place(y, x_peer(j), core, z), device_id_type=MESH,
        )

    def copy_y1(p, a):
        return pltpu.make_async_remote_copy(
            src_ref=qy1.at[p, a], dst_ref=ry1.at[p, a], send_sem=y1s.at[p, a], recv_sem=y1r.at[p, a],
            device_id=place(phase_y(p), x, core, z), device_id_type=MESH,
        )

    def steps_to(h, a):
        return lax.rem(h * 2 + a - x + 4, 4)

    def send1(p, a):
        copy_0(p, a).wait_recv()
        pair[...] = wg[pl.ds(rows_of(p, a, core), 2 * HALF), :] + r0[p, a]
        for h in range(2):
            for k in range(8):
                parted[h, SHARE * k : SHARE * (k + 1), :] = pair[SHARE * (2 * k + h) : SHARE * (2 * k + h + 1), :]
        for h in range(2):
            j = steps_to(h, a)
            coded = encode(parted[h, :, 0:128])

            @pl.when(j != 0)
            def _():
                qx1[p, j - 1] = coded
                copy_x1(p, j).start()

            @pl.when(j == 0)
            def _():
                ownx[p] = parted[h, :, 0:128]

        for h in range(2):
            if p < 3:
                qy1[p, a, h] = encode(parted[h, :, 128:256])
            else:
                owny[a, h] = parted[h, :, 128:256]
        if p < 3:
            go(copy_y1(p, a))

    def copy_x2(p):
        return pltpu.make_async_remote_copy(
            src_ref=qx2.at[p], dst_ref=rx2.at[p], send_sem=x2s.at[p], recv_sem=x2r.at[p],
            device_id=place(phase_y(p), x, core, z), device_id_type=MESH,
        )

    def copy_y2(j):
        return pltpu.make_async_remote_copy(
            src_ref=qy2.at[j - 1], dst_ref=ry2.at[j - 1], send_sem=y2s.at[j - 1], recv_sem=y2r.at[j - 1],
            device_id=place(y, x_peer(j), core, z), device_id_type=MESH,
        )

    def send2x(p):
        v = ownx[p]
        for j in (1, 3, 2):
            copy_x1(p, j).wait_recv()
            v = v + decode(rx1[p, j - 1])
        if p < 3:
            qx2[p] = encode(v)
            go(copy_x2(p))
        else:
            total[0:HALF, 0:128] = v

    def send2y(a):
        for p in range(3):
            copy_y1(p, a).wait_recv()
        for h in range(2):
            j = steps_to(h, a)
            v = owny[a, h]
            for p in range(3):
                v = v + decode(ry1[p, a, h])
            coded = encode(v)

            @pl.when(j != 0)
            def _():
                qy2[j - 1] = coded
                copy_y2(j).start()

            @pl.when(j == 0)
            def _():
                total[0:HALF, 128:256] = v

    row32 = lax.broadcasted_iota(jnp.int32, (32, 256), 0)

    def copy_3(j):
        return pltpu.make_async_remote_copy(
            src_ref=q3.at[z_peer(j)], dst_ref=r3.at[j - 1], send_sem=s3s.at[j - 1], recv_sem=s3r.at[j - 1],
            device_id=place(y, x, core, z_peer(j)), device_id_type=MESH,
        )

    def send3():
        v = total[0:HALF, 0:128]
        for p in range(3):
            copy_x2(p).wait_recv()
            v = v + decode(rx2[p])
        total[0:HALF, 0:128] = v
        v = total[0:HALF, 128:256]
        for j in (1, 2, 3):
            copy_y2(j).wait_recv()
            v = v + decode(ry2[j - 1])
        total[0:HALF, 128:256] = v
        total[HALF:PADDED, :] = jnp.zeros((PADDED - HALF, 256), F32)
        for s in range(8):
            v = jnp.where(row32 < SHARE, total[SHARE * s : SHARE * s + 32, :], 0.0)
            k = exponent(v)
            q = jnp.floor(v * (jnp.exp2(-k) * UNIT) + 0.5)
            q3[s] = jnp.where(row32 < SHARE, q, k).astype(jnp.int32).astype(jnp.int16)
        for j in (4, 3, 5, 2, 6, 1, 7):
            go(copy_3(j))

    def finish():
        def value(q):
            w = q.astype(jnp.int32).astype(F32)
            return w * (jnp.exp2(w[31:32]) * (1.0 / UNIT))

        v = value(q3[z])
        for j in (1, 7, 2, 6, 3, 5, 4):
            copy_3(j).wait_recv()
            v = v + value(r3[j - 1])
        v = v * scale
        wg_ref[pl.ds(0, SHARE, stride=2), :] = v[:SHARE, 0:128]
        wg_ref[pl.ds(1, SHARE, stride=2), :] = v[:SHARE, 128:256]

    keep256 = jnp.where(z_of(256) < 8, 1.0, second)

    stores = []

    def convolve(fr, dst, out, transposed, lo, hi):
        def tile(t, _):
            acc = None
            for o in range(27):
                dx, dy, dz = o // 9, o // 3 % 3, o % 3
                a = fr[dz, pl.ds(2 * t + dx, 2), pl.ds(dy, 8)].reshape(256, 256)
                if transposed:
                    term = lax.dot_general(
                        a, w_all[26 - o], (((1,), (1,)), ((), ())), preferred_element_type=F32
                    )
                else:
                    term = jnp.dot(a, w_all[o], preferred_element_type=F32)
                acc = term if acc is None else acc + term
            dst[pl.ds(2 * t, 2)] = (acc * keep256).astype(BF16).reshape(2, 8, 16, 256)
            return 0

        lax.fori_loop(lo, hi, tile, 0)
        part = pl.ds(2 * lo, 2 * (hi - lo))
        c = pltpu.make_async_copy(dst.at[part], out.at[part], store_sem.at[len(stores)])
        c.start()
        stores.append(c)

    done = 0
    for n, (p, a) in enumerate(PHASES):
        for i in range(done, ENDS[n]):
            gradient(i)
        done = ENDS[n]
        copy_0(p, a).start()
        if n >= 2:
            send1(*PHASES[n - 2])
    send1(*PHASES[6])
    send1(*PHASES[7])
    loads[2].wait()
    convolve(g_fr, ig_ref, ig_hbm, True, 0, 4)
    send2x(0)
    send2x(1)
    near_columns(2, f_halo, f_fr)
    convolve(f_fr, out_ref, out_hbm, False, 0, 1)
    send2y(0)
    send2y(1)
    send2x(2)
    send2x(3)
    send3()
    convolve(f_fr, out_ref, out_hbm, False, 1, 4)
    finish()
    c = pltpu.make_async_copy(wg_ref, wg_hbm, store_sem.at[len(stores)])
    c.start()
    stores.append(c)
    for c in started:
        c.wait_send()
    for p, a in PHASES:
        copy_0(p, a).wait_send()
    for j in (1, 2, 3):
        for p in range(4):
            copy_x1(p, j).wait_send()
        copy_y2(j).wait_send()
    for c in stores:
        c.wait()


def hand_over(a, b, c, a_out, b_out, c_out, a_buf, b_buf, c_buf, in_sems, out_sems):
    moves = [(a, a_buf, a_out, pl.ds(4 * i, 4)) for i in range(2)]
    moves += [(b, b_buf, b_out, pl.ds(4 * i, 4)) for i in range(2)]
    moves += [(c, c_buf, c_out, pl.ds(0, 2 * SHARE))]
    ins = [pltpu.make_async_copy(v.at[part], buf.at[part], in_sems.at[i]) for i, (v, buf, _, part) in enumerate(moves)]
    outs = [pltpu.make_async_copy(buf.at[part], o.at[part], out_sems.at[i]) for i, (_, buf, o, part) in enumerate(moves)]
    for copy in ins:
        copy.start()
    for copy_in, copy_out in zip(ins, outs):
        copy_in.wait()
        copy_out.start()
    for copy in outs:
        copy.wait()


def per_device(features, cotangent, weights, levels, counts):
    f = features.reshape(8, 8, 16, 256)
    g = cotangent.reshape(8, 8, 16, 256)
    scale = 1.0 / math.sqrt(1024 * lax.axis_size("gx") * lax.axis_size("gy"))
    anywhere = pl.BlockSpec(memory_space=pl.ANY)
    dma = pltpu.SemaphoreType.DMA
    i16 = jnp.int16
    out, ig, wgrad = pl.pallas_call(
        functools.partial(kernel, scale),
        out_shape=(
            jax.ShapeDtypeStruct((8, 8, 16, 256), BF16),
            jax.ShapeDtypeStruct((8, 8, 16, 256), BF16),
            jax.ShapeDtypeStruct((2 * SHARE, 128), F32),
        ),
        in_specs=[anywhere] * 5,
        out_specs=(anywhere,) * 3,
        scratch_shapes=[
            pltpu.SMEM((1, 1, 2), jnp.int32),
            pltpu.SMEM((1, 1), jnp.int32),
            pltpu.VMEM((8, 8, 16, 256), BF16),
            pltpu.VMEM((8, 8, 16, 256), BF16),
            pltpu.VMEM((2 * SHARE, 128), F32),
            pltpu.VMEM((8, 8, 16, 256), BF16),
            pltpu.VMEM((8, 8, 16, 256), BF16),
            pltpu.VMEM((27, 256, 256), BF16),
            pltpu.VMEM((3, 10, 10, 16, 256), BF16),
            pltpu.VMEM((3, 10, 10, 16, 256), BF16),
            pltpu.VMEM((36, 16, 256), BF16),
            pltpu.VMEM((36, 16, 256), BF16),
            pltpu.VMEM((8, 256), F32),
            pltpu.VMEM((8, 8, 256), F32),
            pltpu.VMEM((256, 1024), BF16),
            pltpu.VMEM((6912, 256), F32),
            pltpu.VMEM((4, 2, 2 * HALF, 256), F32),
            pltpu.VMEM((2 * HALF, 256), F32),
            pltpu.VMEM((2, HALF, 256), F32),
            pltpu.VMEM((4, 3, PADDED, 128), i16),
            pltpu.VMEM((3, 2, 2, PADDED, 128), i16),
            pltpu.VMEM((4, HALF, 128), F32),
            pltpu.VMEM((2, 2, HALF, 128), F32),
            pltpu.VMEM((4, 3, PADDED, 128), i16),
            pltpu.VMEM((3, 2, 2, PADDED, 128), i16),
            pltpu.VMEM((3, PADDED, 128), i16),
            pltpu.VMEM((3, PADDED, 128), i16),
            pltpu.VMEM((3, PADDED, 128), i16),
            pltpu.VMEM((3, PADDED, 128), i16),
            pltpu.VMEM((PADDED, 256), F32),
            pltpu.VMEM((8, 32, 256), i16),
            pltpu.VMEM((7, 32, 256), i16),
            dma((5,)),
            dma((4,)),
            dma((3, 8)),
            dma((3, 8)),
            dma((4, 2)),
            dma((4, 2)),
            dma((4, 3)),
            dma((4, 3)),
            dma((3, 2)),
            dma((3, 2)),
            dma((3,)),
            dma((3,)),
            dma((3,)),
            dma((3,)),
            dma((7,)),
            dma((7,)),
        ],
        compiler_params=pltpu.CompilerParams(
            collective_id=0, has_side_effects=True, vmem_limit_bytes=56 * 1024 * 1024
        ),
    )(levels, counts, f, g, weights)
    out, ig, wgrad = pl.pallas_call(
        hand_over,
        out_shape=tuple(jax.ShapeDtypeStruct(v.shape, v.dtype) for v in (out, ig, wgrad)),
        in_specs=[anywhere] * 3,
        out_specs=(anywhere,) * 3,
        scratch_shapes=[
            pltpu.VMEM(out.shape, BF16),
            pltpu.VMEM(ig.shape, BF16),
            pltpu.VMEM(wgrad.shape, F32),
            dma((5,)),
            dma((5,)),
        ],
    )(out, ig, wgrad)
    shape = features.shape
    return out.reshape(shape), ig.reshape(shape), wgrad.reshape(-1)


def solution(mesh):
    return jax.shard_map(
        per_device,
        mesh=mesh,
        in_specs=(
            P("gx", "gy", None, None, None),
            P("gx", "gy", None, None, None),
            P(),
            P("gx", "gy", None),
            P("gx", "gy"),
        ),
        out_specs=(
            P("gx", "gy", None, None, None),
            P("gx", "gy", None, None, None),
            P(("gx", "gy")),
        ),
        check_vma=False,
    )
```

```python
import functools
import math

import jax
import jax.numpy as jnp
from jax import lax
from jax.experimental import pallas as pl
from jax.experimental.pallas import tpu as pltpu
from jax.sharding import PartitionSpec as P

F32 = jnp.float32
BF16 = jnp.bfloat16
MESH = pl.DeviceIdType.MESH

DIRS = ((-1, 0), (1, 0), (0, -1), (0, 1), (-1, -1), (-1, 1), (1, -1), (1, 1))
COLS = (0, 8, 16, 24, 32, 33, 34, 35)
WIDE = (8, 8, 8, 8, 1, 1, 1, 1)
PHASES = tuple((p, a) for p in range(4) for a in range(2))
ENDS = (5, 8, 11, 15, 18, 21, 25, 27)
SHARE = 27
HALF = 8 * SHARE
PADDED = 224
UNIT = 32000.0


def up_down(v, top, bottom, z):
    rows = v.shape[0]
    lower = jnp.where(z == 0, bottom, pltpu.roll(v, 1, 0))
    higher = jnp.where(z == 15, top, pltpu.roll(v, rows - 1, 0))
    return lower, higher


def exponent(v):
    peak = jnp.max(jnp.abs(v), axis=0, keepdims=True)
    return jnp.ceil(jnp.log2(jnp.maximum(peak, 1e-30)))


def encode(v):
    k = exponent(v)
    q = jnp.floor(v * (jnp.exp2(-k) * UNIT) + 0.5)
    tail = jnp.broadcast_to(k, (PADDED - HALF, v.shape[1]))
    return jnp.concatenate([q, tail], axis=0).astype(jnp.int32).astype(jnp.int16)


def decode(q):
    w = q.astype(jnp.int32).astype(F32)
    return w[:HALF] * (jnp.exp2(w[HALF : HALF + 1]) * (1.0 / UNIT))


def kernel(
    scale, lev_hbm, cnt_hbm, f_hbm, g_hbm, w_hbm, out_hbm, ig_hbm, wg_hbm,
    lev, cnt, out_ref, ig_ref, wg_ref,
    f_own, g_own, w_all, f_fr, g_fr, f_halo, g_halo, meta, near, ft, wg,
    r0, pair, parted, qx1, qy1, ownx, owny, rx1, ry1, qx2, qy2, rx2, ry2, total, q3, r3,
    load_sem, store_sem, hs, hr, s0s, s0r, x1s, x1r, y1s, y1r, x2s, x2r, y2s, y2r, s3s, s3r,
):
    gx, gy = lax.axis_index("gx"), lax.axis_index("gy")
    y, xl, core = lax.div(gx, 4), lax.rem(lax.div(gx, 2), 2), lax.rem(gx, 2)
    z, xh = lax.div(gy, 2), lax.rem(gy, 2)
    x = xh * 2 + xl

    def place(y_, x_, core_, z_):
        return (y_ * 4 + lax.rem(x_, 2) * 2 + core_, z_ * 2 + lax.div(x_, 2))

    sibling = place(y, x, 1 - core, z)

    def x_peer(j):
        return lax.rem(x + j, 4)

    def y_peer(j):
        return lax.rem(y + j, 4)

    def z_peer(j):
        return lax.rem(z + j, 8)

    def neighbour(d):
        return (lax.rem(gx + d[0] + 16, 16), lax.rem(gy + d[1] + 16, 16))

    loads = [
        pltpu.make_async_copy(g_hbm, g_own, load_sem.at[0]),
        pltpu.make_async_copy(f_hbm, f_own, load_sem.at[1]),
        pltpu.make_async_copy(w_hbm, w_all, load_sem.at[2]),
        pltpu.make_async_copy(lev_hbm, lev, load_sem.at[3]),
        pltpu.make_async_copy(cnt_hbm, cnt, load_sem.at[4]),
    ]

    barrier = pltpu.get_barrier_semaphore()
    def greet(device):
        pl.semaphore_signal(barrier, inc=1, device_id=device, device_id_type=MESH)

    greet(place(y, x, core, z_peer(4)))
    for i in (4, 5, 6, 7):
        greet(neighbour(DIRS[i]))
    for i in (2, 3):
        greet(neighbour(DIRS[i]))
    for j in (3, 5, 2, 6):
        greet(place(y, x, core, z_peer(j)))
    for j in (2, 1, 3):
        greet(place(y, x_peer(j), core, z))
        greet(place(y_peer(j), x, core, z))
    for j in (1, 7):
        greet(place(y, x, core, z_peer(j)))
    for i in (0, 1):
        greet(neighbour(DIRS[i]))
    greet(sibling)
    for n in (3, 4, 0, 1, 2):
        loads[n].start()
    loads[3].wait()
    loads[4].wait()

    shift = lev[0, 0, 0].astype(F32)
    second = jnp.where(cnt[0, 0] >= 2, 1.0, 0.0).astype(F32)
    meta[...] = jnp.where(lax.broadcasted_iota(jnp.int32, (2, 128), 0) == 0, shift, second)
    loads[0].wait()
    loads[1].wait()
    pl.semaphore_wait(barrier, 22)

    def edge(ref, d):
        row = {-1: 0, 1: 7}
        if d[0] and d[1]:
            return ref.at[row[d[0]], row[d[1]]]
        return ref.at[row[d[0]]] if d[0] else ref.at[:, row[d[1]]]

    def slot(ref, i):
        return ref.at[COLS[i]] if WIDE[i] == 1 else ref.at[pl.ds(COLS[i], 8)]

    def halo(kind, i):
        d = DIRS[i]
        opposite = DIRS.index((-d[0], -d[1]))
        if kind == 0:
            src, dst = meta, near.at[opposite]
        else:
            src = edge((None, g_own, f_own)[kind], d)
            dst = slot((None, g_halo, f_halo)[kind], opposite)
        return pltpu.make_async_remote_copy(
            src_ref=src, dst_ref=dst, send_sem=hs.at[kind, i], recv_sem=hr.at[kind, opposite],
            device_id=neighbour(d), device_id_type=MESH,
        )

    started = []

    def go(copy):
        copy.start()
        started.append(copy)

    for i in (4, 5, 6, 7, 2, 3, 0, 1):
        go(halo(0, i))
        go(halo(1, i))

    def z_of(rows):
        return lax.rem(lax.broadcasted_iota(jnp.int32, (rows, 256), 0), 16)

    z128 = z_of(128)
    keep128 = jnp.where(z128 < 8, 1.0, second)

    def own_columns(src, fr, with_transpose):
        for r in range(8):
            v = src[r].reshape(128, 256).astype(F32) * keep128
            lower, higher = up_down(v, 0.0, 0.0, z128)
            for k, t in enumerate((lower, v, higher)):
                fr[k, r + 1, 1:9] = t.astype(BF16).reshape(8, 16, 256)
            if with_transpose:
                ft[:, r * 128 : (r + 1) * 128] = v.T.astype(BF16)

    own_columns(g_own, g_fr, False)
    own_columns(f_own, f_fr, True)

    def near_columns(kind, recv, fr):
        for i in (0, 1, 4, 5, 6, 7, 2, 3):
            dx, dy = DIRS[i]
            if kind == 1:
                halo(0, DIRS.index((-dx, -dy))).wait_recv()
            halo(kind, DIRS.index((-dx, -dy))).wait_recv()
            n = WIDE[i]
            inside = jnp.logical_and(
                jnp.logical_and(gx + dx >= 0, gx + dx < 16), jnp.logical_and(gy + dy >= 0, gy + dy < 16)
            )
            valid = jnp.where(inside, 1.0, 0.0).astype(F32)
            facts = jnp.concatenate([near[i], near[i]], axis=1)
            higher_by = facts[0:1] - shift
            level = jnp.where(higher_by == 0.0, valid, 0.0)
            above = jnp.where(higher_by == 1.0, valid, 0.0)
            below = jnp.where(higher_by == -1.0, valid, 0.0)
            rows = n * 16
            zr = z_of(rows)
            v = recv[COLS[i] : COLS[i] + n].reshape(rows, 256).astype(F32)
            v = v * jnp.where(zr < 8, 1.0, facts[1:2])
            swapped = pltpu.roll(v, 8, 0) if n == 1 else None
            up8 = swapped if n == 1 else pltpu.roll(v, 8, 0)
            down8 = swapped if n == 1 else pltpu.roll(v, rows - 8, 0)
            c = level * v + jnp.where(zr >= 8, above * up8, below * down8)
            top = above * pltpu.roll(v, 7, 0)
            bottom = below * pltpu.roll(v, rows - 7, 0)
            lower, higher = up_down(c, top, bottom, zr)
            xs = {-1: 0, 0: slice(1, 9), 1: 9}[dx]
            ys = {-1: 0, 0: slice(1, 9), 1: 9}[dy]
            for k, t in enumerate((lower, c, higher)):
                t = t.astype(BF16)
                fr[k, xs, ys] = t if n == 1 else t.reshape(8, 16, 256)

    near_columns(1, g_halo, g_fr)
    for i in range(8):
        go(halo(2, i))

    first = y_peer(1)
    base = lax.div(27 * first, 4)

    def gradient(i):
        o = lax.rem(base + i, 27)
        dx, dy, dz = lax.div(o, 9), lax.rem(lax.div(o, 3), 3), lax.rem(o, 3)
        g = g_fr[2 - dz, pl.ds(2 - dx, 8), pl.ds(2 - dy, 8)].reshape(1024, 256)
        wg[pl.ds(pl.multiple_of(o * 256, 256), 256), :] = jnp.dot(ft[...], g, preferred_element_type=F32)

    def phase_y(p):
        return lax.rem(y + 1 + p, 4)

    def rows_of(p, xl_, core_):
        return pl.multiple_of(((phase_y(p) * 2 + xl_) * 2 + core_) * (2 * HALF), 8)

    def copy_0(p, a):
        return pltpu.make_async_remote_copy(
            src_ref=wg.at[pl.ds(rows_of(p, a, 1 - core), 2 * HALF)], dst_ref=r0.at[p, a],
            send_sem=s0s.at[p, a], recv_sem=s0r.at[p, a], device_id=sibling, device_id_type=MESH,
        )

    def copy_x1(p, j):
        return pltpu.make_async_remote_copy(
            src_ref=qx1.at[p, j - 1], dst_ref=rx1.at[p, j - 1], send_sem=x1s.at[p, j - 1],
            recv_sem=x1r.at[p, j - 1], device_id=place(y, x_peer(j), core, z), device_id_type=MESH,
        )

    def copy_y1(p, a):
        return pltpu.make_async_remote_copy(
            src_ref=qy1.at[p, a], dst_ref=ry1.at[p, a], send_sem=y1s.at[p, a], recv_sem=y1r.at[p, a],
            device_id=place(phase_y(p), x, core, z), device_id_type=MESH,
        )

    def steps_to(h, a):
        return lax.rem(h * 2 + a - x + 4, 4)

    def send1(p, a):
        copy_0(p, a).wait_recv()
        pair[...] = wg[pl.ds(rows_of(p, a, core), 2 * HALF), :] + r0[p, a]
        for h in range(2):
            for k in range(8):
                parted[h, SHARE * k : SHARE * (k + 1), :] = pair[SHARE * (2 * k + h) : SHARE * (2 * k + h + 1), :]
        for h in range(2):
            j = steps_to(h, a)
            coded = encode(parted[h, :, 0:128])

            @pl.when(j != 0)
            def _():
                qx1[p, j - 1] = coded
                copy_x1(p, j).start()

            @pl.when(j == 0)
            def _():
                ownx[p] = parted[h, :, 0:128]

        for h in range(2):
            if p < 3:
                qy1[p, a, h] = encode(parted[h, :, 128:256])
            else:
                owny[a, h] = parted[h, :, 128:256]
        if p < 3:
            go(copy_y1(p, a))

    def copy_x2(p):
        return pltpu.make_async_remote_copy(
            src_ref=qx2.at[p], dst_ref=rx2.at[p], send_sem=x2s.at[p], recv_sem=x2r.at[p],
            device_id=place(phase_y(p), x, core, z), device_id_type=MESH,
        )

    def copy_y2(j):
        return pltpu.make_async_remote_copy(
            src_ref=qy2.at[j - 1], dst_ref=ry2.at[j - 1], send_sem=y2s.at[j - 1], recv_sem=y2r.at[j - 1],
            device_id=place(y, x_peer(j), core, z), device_id_type=MESH,
        )

    def send2x(p):
        v = ownx[p]
        for j in (1, 3, 2):
            copy_x1(p, j).wait_recv()
            v = v + decode(rx1[p, j - 1])
        if p < 3:
            qx2[p] = encode(v)
            go(copy_x2(p))
        else:
            total[0:HALF, 0:128] = v

    def send2y(a):
        for p in range(3):
            copy_y1(p, a).wait_recv()
        for h in range(2):
            j = steps_to(h, a)
            v = owny[a, h]
            for p in range(3):
                v = v + decode(ry1[p, a, h])
            coded = encode(v)

            @pl.when(j != 0)
            def _():
                qy2[j - 1] = coded
                copy_y2(j).start()

            @pl.when(j == 0)
            def _():
                total[0:HALF, 128:256] = v

    row32 = lax.broadcasted_iota(jnp.int32, (32, 256), 0)

    def copy_3(j):
        return pltpu.make_async_remote_copy(
            src_ref=q3.at[z_peer(j)], dst_ref=r3.at[j - 1], send_sem=s3s.at[j - 1], recv_sem=s3r.at[j - 1],
            device_id=place(y, x, core, z_peer(j)), device_id_type=MESH,
        )

    def send3():
        v = total[0:HALF, 0:128]
        for p in range(3):
            copy_x2(p).wait_recv()
            v = v + decode(rx2[p])
        total[0:HALF, 0:128] = v
        v = total[0:HALF, 128:256]
        for j in (1, 2, 3):
            copy_y2(j).wait_recv()
            v = v + decode(ry2[j - 1])
        total[0:HALF, 128:256] = v
        total[HALF:PADDED, :] = jnp.zeros((PADDED - HALF, 256), F32)
        for s in range(8):
            v = jnp.where(row32 < SHARE, total[SHARE * s : SHARE * s + 32, :], 0.0)
            k = exponent(v)
            q = jnp.floor(v * (jnp.exp2(-k) * UNIT) + 0.5)
            q3[s] = jnp.where(row32 < SHARE, q, k).astype(jnp.int32).astype(jnp.int16)
        for j in (4, 3, 5, 2, 6, 1, 7):
            go(copy_3(j))

    def finish():
        def value(q):
            w = q.astype(jnp.int32).astype(F32)
            return w * (jnp.exp2(w[31:32]) * (1.0 / UNIT))

        v = value(q3[z])
        for j in (1, 7, 2, 6, 3, 5, 4):
            copy_3(j).wait_recv()
            v = v + value(r3[j - 1])
        v = v * scale
        wg_ref[pl.ds(0, SHARE, stride=2), :] = v[:SHARE, 0:128]
        wg_ref[pl.ds(1, SHARE, stride=2), :] = v[:SHARE, 128:256]

    keep256 = jnp.where(z_of(256) < 8, 1.0, second)

    stores = []

    def convolve(fr, dst, out, transposed, lo, hi):
        def tile(t, _):
            acc = None
            for o in range(27):
                dx, dy, dz = o // 9, o // 3 % 3, o % 3
                a = fr[dz, pl.ds(2 * t + dx, 2), pl.ds(dy, 8)].reshape(256, 256)
                if transposed:
                    term = lax.dot_general(
                        a, w_all[26 - o], (((1,), (1,)), ((), ())), preferred_element_type=F32
                    )
                else:
                    term = jnp.dot(a, w_all[o], preferred_element_type=F32)
                acc = term if acc is None else acc + term
            dst[pl.ds(2 * t, 2)] = (acc * keep256).astype(BF16).reshape(2, 8, 16, 256)
            return 0

        lax.fori_loop(lo, hi, tile, 0)
        part = pl.ds(2 * lo, 2 * (hi - lo))
        c = pltpu.make_async_copy(dst.at[part], out.at[part], store_sem.at[len(stores)])
        c.start()
        stores.append(c)

    done = 0
    for n, (p, a) in enumerate(PHASES):
        for i in range(done, ENDS[n]):
            gradient(i)
        done = ENDS[n]
        copy_0(p, a).start()
        if n >= 2:
            send1(*PHASES[n - 2])
    send1(*PHASES[6])
    send1(*PHASES[7])
    loads[2].wait()
    convolve(g_fr, ig_ref, ig_hbm, True, 0, 4)
    send2x(0)
    send2x(1)
    near_columns(2, f_halo, f_fr)
    convolve(f_fr, out_ref, out_hbm, False, 0, 1)
    send2y(0)
    send2y(1)
    send2x(2)
    send2x(3)
    send3()
    convolve(f_fr, out_ref, out_hbm, False, 1, 4)
    finish()
    c = pltpu.make_async_copy(wg_ref, wg_hbm, store_sem.at[len(stores)])
    c.start()
    stores.append(c)
    for c in started:
        c.wait_send()
    for p, a in PHASES:
        copy_0(p, a).wait_send()
    for j in (1, 2, 3):
        for p in range(4):
            copy_x1(p, j).wait_send()
        copy_y2(j).wait_send()
    for c in stores:
        c.wait()


def hand_over(a, b, c, a_out, b_out, c_out, a_buf, b_buf, c_buf, in_sems, out_sems):
    moves = [(a, a_buf, a_out, pl.ds(4 * i, 4)) for i in range(2)]
    moves += [(b, b_buf, b_out, pl.ds(4 * i, 4)) for i in range(2)]
    moves += [(c, c_buf, c_out, pl.ds(0, 2 * SHARE))]
    ins = [pltpu.make_async_copy(v.at[part], buf.at[part], in_sems.at[i]) for i, (v, buf, _, part) in enumerate(moves)]
    outs = [pltpu.make_async_copy(buf.at[part], o.at[part], out_sems.at[i]) for i, (_, buf, o, part) in enumerate(moves)]
    for copy in ins:
        copy.start()
    for copy_in, copy_out in zip(ins, outs):
        copy_in.wait()
        copy_out.start()
    for copy in outs:
        copy.wait()


def per_device(features, cotangent, weights, levels, counts):
    f = features.reshape(8, 8, 16, 256)
    g = cotangent.reshape(8, 8, 16, 256)
    scale = 1.0 / math.sqrt(1024 * lax.axis_size("gx") * lax.axis_size("gy"))
    anywhere = pl.BlockSpec(memory_space=pl.ANY)
    dma = pltpu.SemaphoreType.DMA
    i16 = jnp.int16
    out, ig, wgrad = pl.pallas_call(
        functools.partial(kernel, scale),
        out_shape=(
            jax.ShapeDtypeStruct((8, 8, 16, 256), BF16),
            jax.ShapeDtypeStruct((8, 8, 16, 256), BF16),
            jax.ShapeDtypeStruct((2 * SHARE, 128), F32),
        ),
        in_specs=[anywhere] * 5,
        out_specs=(anywhere,) * 3,
        scratch_shapes=[
            pltpu.SMEM((1, 1, 2), jnp.int32),
            pltpu.SMEM((1, 1), jnp.int32),
            pltpu.VMEM((8, 8, 16, 256), BF16),
            pltpu.VMEM((8, 8, 16, 256), BF16),
            pltpu.VMEM((2 * SHARE, 128), F32),
            pltpu.VMEM((8, 8, 16, 256), BF16),
            pltpu.VMEM((8, 8, 16, 256), BF16),
            pltpu.VMEM((27, 256, 256), BF16),
            pltpu.VMEM((3, 10, 10, 16, 256), BF16),
            pltpu.VMEM((3, 10, 10, 16, 256), BF16),
            pltpu.VMEM((36, 16, 256), BF16),
            pltpu.VMEM((36, 16, 256), BF16),
            pltpu.VMEM((2, 128), F32),
            pltpu.VMEM((8, 2, 128), F32),
            pltpu.VMEM((256, 1024), BF16),
            pltpu.VMEM((6912, 256), F32),
            pltpu.VMEM((4, 2, 2 * HALF, 256), F32),
            pltpu.VMEM((2 * HALF, 256), F32),
            pltpu.VMEM((2, HALF, 256), F32),
            pltpu.VMEM((4, 3, PADDED, 128), i16),
            pltpu.VMEM((3, 2, 2, PADDED, 128), i16),
            pltpu.VMEM((4, HALF, 128), F32),
            pltpu.VMEM((2, 2, HALF, 128), F32),
            pltpu.VMEM((4, 3, PADDED, 128), i16),
            pltpu.VMEM((3, 2, 2, PADDED, 128), i16),
            pltpu.VMEM((3, PADDED, 128), i16),
            pltpu.VMEM((3, PADDED, 128), i16),
            pltpu.VMEM((3, PADDED, 128), i16),
            pltpu.VMEM((3, PADDED, 128), i16),
            pltpu.VMEM((PADDED, 256), F32),
            pltpu.VMEM((8, 32, 256), i16),
            pltpu.VMEM((7, 32, 256), i16),
            dma((5,)),
            dma((4,)),
            dma((3, 8)),
            dma((3, 8)),
            dma((4, 2)),
            dma((4, 2)),
            dma((4, 3)),
            dma((4, 3)),
            dma((3, 2)),
            dma((3, 2)),
            dma((3,)),
            dma((3,)),
            dma((3,)),
            dma((3,)),
            dma((7,)),
            dma((7,)),
        ],
        compiler_params=pltpu.CompilerParams(
            collective_id=0, has_side_effects=True, vmem_limit_bytes=56 * 1024 * 1024
        ),
    )(levels, counts, f, g, weights)
    out, ig, wgrad = pl.pallas_call(
        hand_over,
        out_shape=tuple(jax.ShapeDtypeStruct(v.shape, v.dtype) for v in (out, ig, wgrad)),
        in_specs=[anywhere] * 3,
        out_specs=(anywhere,) * 3,
        scratch_shapes=[
            pltpu.VMEM(out.shape, BF16),
            pltpu.VMEM(ig.shape, BF16),
            pltpu.VMEM(wgrad.shape, F32),
            dma((5,)),
            dma((5,)),
        ],
    )(out, ig, wgrad)
    shape = features.shape
    return out.reshape(shape), ig.reshape(shape), wgrad.reshape(-1)


def solution(mesh):
    return jax.shard_map(
        per_device,
        mesh=mesh,
        in_specs=(
            P("gx", "gy", None, None, None),
            P("gx", "gy", None, None, None),
            P(),
            P("gx", "gy", None),
            P("gx", "gy"),
        ),
        out_specs=(
            P("gx", "gy", None, None, None),
            P("gx", "gy", None, None, None),
            P(("gx", "gy")),
        ),
        check_vma=False,
    )
```
